512 devices in a mesh: wide: 128 (over x, z, core), narrow: 4 (over y).
Axes of the slice: x: 4, y: 4, z: 16, core: 2. Of those that a mesh axis runs over, the one named last changes fastest.
Arguments:
- positions: float32 [3, 1048576], P(None, ('wide', 'narrow')), as said below
- directions: float32 [3, 1048576], P(None, ('wide', 'narrow')), may hold values from -0.6 to 0.6
- radius: float32 [1048576], P(('wide', 'narrow')), may hold values from 0.01 to 0.05
- currents: float32 [16, 1048576], P(None, ('wide', 'narrow')), may hold values from -6 to 6
- pair_target: int32 [4096, 32], P(('wide', 'narrow')), may hold values from 0 to 223, as said below
- pair_count: int32 [4096], P(('wide', 'narrow')), may hold values from 1 to 32
Outputs:
- voltages: float32 [16, 1048576], P(None, ('wide', 'narrow'))
The draws below stay inside these ranges and needn't reach their ends.
Inputs may be any that keep to these rules, and one draw needn't show every extreme that they name: The partner slab i // 32 + pair_target[i, s] // 32 exists for every slot, used or not. `positions`: the third coordinate of a filament whose block lies in slab s is between 0.1 * s and 0.1 * (s + 2).
All inputs are finite; a program needn't handle non-finite values.
Results may differ from the reference program's by a relative error of at most 0.0029.
Values sent between devices are 32-bit elements; how exact they have to be, the bound alone decides.
A program may use at most 128 MiB of HBM per device.

```python
import math
import jax
import jax.numpy as jnp
from jax import lax

FIL = 256
PORTS = 16
BLK_DEV = 8
MAXP = 32
REACH = 6
SLAB_BLK = 32
BLOCKS = 4096
FILS = 1048576


def draw_positions(key, part):
    key = jax.random.fold_in(key, 12)
    first, second = jax.random.split(key)
    slab = (jnp.arange(FILS) // (SLAB_BLK * FIL)).astype(jnp.float32)
    plane = jax.random.uniform(first, (2, FILS), jnp.float32)
    depth = 2.0 * jax.random.uniform(second, (FILS,), jnp.float32)
    height = 0.1 * (slab + depth)
    return jnp.concatenate([plane, height[None, :]], axis=0).astype(jnp.float32)


def draw_pair_target(key, part):
    key = jax.random.fold_in(key, 13)
    first, second = jax.random.split(key)
    slabs = BLOCKS // SLAB_BLK
    slab = jnp.arange(BLOCKS, dtype=jnp.int32) // SLAB_BLK
    top = jnp.minimum(REACH, slabs - 1 - slab)
    offset = jax.random.randint(first, (BLOCKS, MAXP), 0, REACH + 1) % (top[:, None] + 1)
    member = jax.random.randint(second, (BLOCKS, MAXP), 0, SLAB_BLK)
    target = offset * SLAB_BLK + member
    target = target.at[0, 0].set(REACH * SLAB_BLK + SLAB_BLK - 1)
    target = target.at[0, 1].set(0)
    return target.astype(jnp.int32)


def draw_pair_count(key, part):
    key = jax.random.fold_in(key, 14)
    first, second, third, fourth = jax.random.split(key, 4)
    devices = BLOCKS // BLK_DEV
    heavy = jax.random.randint(first, (devices,), 0, 4) == 0
    heavy = jnp.repeat(heavy, BLK_DEV)
    light = jax.random.randint(second, (BLOCKS,), 3 * MAXP // 8, 5 * MAXP // 8 + 1)
    busy = jax.random.randint(third, (BLOCKS,), 3 * MAXP // 4, MAXP + 1)
    count = jnp.where(heavy, busy, light)
    chosen = jax.random.randint(fourth, (), 0, BLOCKS)
    count = count.at[chosen].set(MAXP)
    return count.astype(jnp.int32)


def level_of(rng, dims, pieces, least, largest):
    level, own = 1.0, jax.random.fold_in(rng, 6)
    for position, shards_of in pieces:
        draws = jnp.exp(jax.random.uniform(jax.random.fold_in(own, position), (shards_of,), jnp.float32, least / len(pieces), largest / len(pieces)))
        level = level * jnp.repeat(draws, dims[position] // shards_of).reshape([-1 if axis == position else 1 for axis in range(len(dims))])
    return level


def noise(rng, extent, width, bound, cuts=(), held_as=jnp.bfloat16):
    factor_of = level_of(rng, extent, cuts, -0.22, 0.18) if cuts else 1.0
    array = jax.random.normal(rng, extent, jnp.float32) * width * factor_of
    return jnp.minimum(jnp.maximum(array, -bound), bound).astype(held_as)


def setup_inputs(seed: int = 0) -> dict:
    splits = jax.random.split(jax.random.key(seed), 7)
    positions = draw_positions(jax.random.fold_in(splits[6], 71), 0)
    directions = noise(splits[1], (3, FILS), 0.1, 0.6, ((1, 512),), jnp.float32)
    radius = jnp.clip(jnp.exp(math.log(0.05) - 1.609438 * jax.random.uniform(splits[2], (FILS,), jnp.float32) ** level_of(splits[2], (FILS,), ((0, 512),), -0.2, 0.2)), 0.01, 0.05)
    currents = noise(splits[3], (PORTS, FILS), 1.0, 6.0, ((1, 512),), jnp.float32)
    pair_target = draw_pair_target(jax.random.fold_in(splits[6], 71), 0)
    pair_count = draw_pair_count(jax.random.fold_in(splits[6], 71), 0)
    return dict(positions=positions, directions=directions, radius=radius, currents=currents, pair_target=pair_target, pair_count=pair_count)


def kernel_tile(pos_a, dir_a, rad_a, pos_b, dir_b, rad_b):
    gap = rad_a[..., :, None] ** 2 + rad_b[..., None, :] ** 2
    along = jnp.zeros_like(gap)
    for comp in range(3):
        diff = pos_a[comp][..., :, None] - pos_b[comp][..., None, :]
        gap = gap + diff * diff
        along = along + dir_a[comp][..., :, None] * dir_b[comp][..., None, :]
    rounded = lax.optimization_barrier((along / jnp.sqrt(gap)).astype(jnp.bfloat16))
    return rounded.astype(jnp.float32)

def reference(positions, directions, radius, currents, pair_target, pair_count):
    high = lax.Precision.HIGHEST

    def cut(arr, index):
        return lax.dynamic_slice_in_dim(arr, (index * FIL).astype(jnp.int32), FIL, arr.ndim - 1)

    def block_tile(first, second):
        return kernel_tile(cut(positions, first), cut(directions, first), cut(radius, first), cut(positions, second), cut(directions, second), cut(radius, second))

    def diag_block(index):
        tile = block_tile(index, index)
        return lax.dot_general(cut(currents, index), tile, (((1,), (1,)), ((), ())), precision=high, preferred_element_type=jnp.float32)
    diag = lax.map(diag_block, jnp.arange(BLOCKS, dtype=jnp.int32))
    voltages = jnp.transpose(diag, (1, 0, 2)).reshape(PORTS, BLOCKS * FIL)

    def slot(acc, flat):
        source = (flat // MAXP).astype(jnp.int32)
        place = (flat % MAXP).astype(jnp.int32)
        target = pair_target[source, place]
        partner = ((source // SLAB_BLK + target // SLAB_BLK) * SLAB_BLK + target % SLAB_BLK).astype(jnp.int32)

        def add_pair(values):
            tile = block_tile(source, partner)
            ahead = lax.dot_general(cut(currents, partner), tile, (((1,), (1,)), ((), ())), precision=high, preferred_element_type=jnp.float32)
            values = lax.dynamic_update_slice_in_dim(values, cut(values, source) + ahead, (source * FIL).astype(jnp.int32), 1)
            behind = jnp.dot(cut(currents, source), tile, precision=high, preferred_element_type=jnp.float32)
            values = lax.dynamic_update_slice_in_dim(values, cut(values, partner) + behind, (partner * FIL).astype(jnp.int32), 1)
            return values

        def keep(values):
            return values
        return (lax.cond(place < pair_count[source], add_pair, keep, acc), None)
    voltages, _ = lax.scan(slot, voltages, jnp.arange(BLOCKS * MAXP, dtype=jnp.int32))
    return voltages
```

```python
import functools

import jax
import jax.numpy as jnp
from jax import lax
from jax.experimental import pallas as pl
from jax.experimental.pallas import tpu as pltpu
from jax.sharding import PartitionSpec as P

FIL = 256
PORTS = 16
BLK = 8
MAXP = 32
SLAB = 32
MEMBERS = 4
HOPS = 4
ROWS = 24
WINDOW = 2 * HOPS * BLK
LIST = 40 * 32
UNROLL = 8
PARTS = 2
f32 = jnp.float32
bf16 = jnp.bfloat16
MESH = pl.DeviceIdType.MESH


def place():
    wide = lax.axis_index("wide")
    member = lax.axis_index("narrow")
    count = lax.axis_size("wide")
    core = lax.rem(wide, 2)
    twin = wide + 1 - 2 * core
    ahead = lax.rem(wide + 2, count)
    behind = lax.rem(wide + count - 2, count)
    return wide, member, core, twin, ahead, behind


def greet(devices):
    barrier = pltpu.get_barrier_semaphore()
    for device in devices:
        pl.semaphore_signal(barrier, inc=1, device_id=device, device_id_type=MESH)
    pl.semaphore_wait(barrier, len(devices))


def remote(src, dst, send, recv, device):
    return pltpu.make_async_remote_copy(
        src_ref=src, dst_ref=dst, send_sem=send, recv_sem=recv, device_id=device, device_id_type=MESH
    )


def list_pairs(rows, member, core, li_ref, lj_ref):
    lane = lax.broadcasted_iota(jnp.int32, (8, FIL), 1)
    row = lax.broadcasted_iota(jnp.int32, (8, FIL), 0)
    mine = (rows >= 0) & ((rows & 31) // BLK == member)
    hit = mine.astype(bf16)
    upper = (
        lax.broadcasted_iota(jnp.int32, (FIL, FIL), 0) <= lax.broadcasted_iota(jnp.int32, (FIL, FIL), 1)
    ).astype(bf16)
    inclusive = jnp.dot(hit, upper, preferred_element_type=f32).astype(jnp.int32)
    totals = jnp.sum(mine.astype(jnp.int32), axis=1, keepdims=True)
    base = jnp.full((8, 1), BLK, jnp.int32)
    which = lax.broadcasted_iota(jnp.int32, (8, 1), 0)
    for m in range(MEMBERS - 1):
        base = base + jnp.where(which > m, totals[m : m + 1], 0)
    spot = jnp.where(mine, base + inclusive - 1, -1)
    source = row * BLK + lane // MAXP
    partner = (core + rows // SLAB) * BLK + (rows & 7)
    high = jnp.where(mine, spot // 32, -1)
    low = jnp.where(mine, spot & 31, -1)
    out_i = jnp.zeros((40, 32), f32)
    out_j = jnp.zeros((40, 32), f32)
    spots_high = lax.broadcasted_iota(jnp.int32, (40, FIL), 0)
    spots_low = lax.broadcasted_iota(jnp.int32, (32, FIL), 0)
    contract = (((1,), (1,)), ((), ()))
    for m in range(MEMBERS):
        pick_high = spots_high == high[m : m + 1]
        pick_low = (spots_low == low[m : m + 1]).astype(f32).astype(bf16)
        put_i = jnp.where(pick_high, source[m : m + 1].astype(f32), 0.0).astype(bf16)
        put_j = jnp.where(pick_high, partner[m : m + 1].astype(f32), 0.0).astype(bf16)
        out_i = out_i + lax.dot_general(put_i, pick_low, contract, preferred_element_type=f32)
        out_j = out_j + lax.dot_general(put_j, pick_low, contract, preferred_element_type=f32)
    total = BLK + jnp.sum(totals[0:MEMBERS], axis=0, keepdims=True)
    flat = 32 * lax.broadcasted_iota(jnp.int32, (40, 32), 0) + lax.broadcasted_iota(jnp.int32, (40, 32), 1)
    diagonal = flat < BLK
    used = flat < total
    li = jnp.where(diagonal, member * BLK + flat, jnp.where(used, out_i.astype(jnp.int32), SLAB))
    lj = jnp.where(diagonal, 2 * WINDOW + core * BLK + flat, jnp.where(used, out_j.astype(jnp.int32), WINDOW))
    li_ref[...] = li
    lj_ref[...] = lj
    return total


def fetch_kernel(
    pos, dirs, rad, cur, pairs, src, par, li_ref, lj_ref, n_ref,
    own, lists, y_send, y_recv, l_send, l_recv, z_send, z_recv, c_send, c_recv, home_sem,
):
    wide, member, core, twin, ahead, behind = place()
    mates = [lax.rem(member + step, MEMBERS) for step in range(1, MEMBERS)]
    lists[...] = jnp.full((8, FIL), -1, jnp.int32)
    lists[pl.ds(member, 1)] = pairs[...]
    greet([(wide, mate) for mate in mates] + [(ahead, member), (twin, member)])
    for b in range(BLK):
        cut = slice(b * FIL, (b + 1) * FIL)
        own[b, 0:3] = pos[:, cut]
        own[b, 3:6] = dirs[:, cut]
        own[b, 6:7] = rad[:, cut]
        own[b, 7:8] = rad[:, cut]
        own[b, 8:ROWS] = cur[:, cut]
    half = BLK // PARTS

    def seat(hop, part):
        return pl.ds((2 * hop + core) * BLK + part * half, half)

    sends = []
    first = []
    for part in range(PARTS):
        copy = remote(
            own.at[pl.ds(part * half, half)], par.at[seat(1, part)], z_send.at[0, part], z_recv.at[0, part], (behind, member)
        )
        copy.start()
        first.append(copy)
    hops = [first]
    list_copies = []
    for step, mate in enumerate(mates):
        copy = remote(
            pairs, lists.at[pl.ds(member, 1)], l_send.at[step], l_recv.at[step], (wide, mate)
        )
        copy.start()
        list_copies.append(copy)
    unit_copies = []
    for step, mate in enumerate(mates):
        copy = remote(own, src.at[pl.ds(member * BLK, BLK)], y_send.at[step], y_recv.at[step], (wide, mate))
        copy.start()
        unit_copies.append(copy)
    core_copies = []
    copy = remote(own, par.at[pl.ds(core * BLK, BLK)], c_send.at[0, 0], c_recv.at[0, 0], (twin, member))
    copy.start()
    core_copies.append(copy)
    home = [
        pltpu.make_async_copy(own, src.at[pl.ds(member * BLK, BLK)], home_sem.at[0]),
        pltpu.make_async_copy(own, par.at[pl.ds(core * BLK, BLK)], home_sem.at[1]),
    ]
    for copy in home:
        copy.start()
    for copy in list_copies:
        copy.wait()
    total = list_pairs(lists[...], member, core, li_ref, lj_ref)
    n_ref[...] = jnp.broadcast_to(total, (8, 128))
    for hop in range(1, HOPS):
        later = []
        for part in range(PARTS):
            hops[hop - 1][part].wait_recv()
            if hop < HOPS - 1:
                copy = remote(
                    par.at[seat(hop, part)], par.at[seat(hop + 1, part)], z_send.at[hop, part], z_recv.at[hop, part], (behind, member)
                )
                copy.start()
                later.append(copy)
            copy = remote(
                par.at[seat(hop, part)], par.at[seat(hop, part)], c_send.at[hop, part], c_recv.at[hop, part], (twin, member)
            )
            copy.start()
            core_copies.append(copy)
        hops.append(later)
    for group in hops:
        for copy in group:
            copy.wait_send()
    for copy in unit_copies + core_copies + home:
        copy.wait()


def fetch(pos, dirs, rad, cur, pairs):
    vm = pl.BlockSpec(memory_space=pltpu.VMEM)
    hbm = pl.BlockSpec(memory_space=pl.ANY)
    dma = pltpu.SemaphoreType.DMA
    return pl.pallas_call(
        fetch_kernel,
        out_shape=[
            jax.ShapeDtypeStruct((SLAB, ROWS, FIL), f32),
            jax.ShapeDtypeStruct((WINDOW, ROWS, FIL), f32),
            jax.ShapeDtypeStruct((40, 32), jnp.int32),
            jax.ShapeDtypeStruct((40, 32), jnp.int32),
            jax.ShapeDtypeStruct((8, 128), jnp.int32),
        ],
        in_specs=[vm] * 5,
        out_specs=[hbm, hbm, vm, vm, vm],
        scratch_shapes=[
            pltpu.VMEM((BLK, ROWS, FIL), f32),
            pltpu.VMEM((8, FIL), jnp.int32),
            dma((3,)), dma((3,)), dma((3,)), dma((3,)),
            dma((3, PARTS)), dma((3, PARTS)),
            dma((HOPS, PARTS)), dma((HOPS, PARTS)),
            dma((2,)),
        ],
        compiler_params=pltpu.CompilerParams(
            collective_id=0, has_side_effects=True, vmem_limit_bytes=32 * 2**20
        ),
    )(pos, dirs, rad, cur, pairs)


def directed(block):
    cur = block[8:ROWS]
    parts = jnp.concatenate([block[3 + comp : 4 + comp] * cur for comp in range(3)], axis=0)
    head = parts.astype(bf16)
    tail = (parts - head.astype(f32)).astype(bf16)
    return jnp.concatenate([head, tail], axis=0)


def tiles_kernel(n_ref, li_ref, lj_ref, src, par, s_out, p_out, c_src, c_par, cols, even, odd):
    n = n_ref[0, 0]

    @pl.loop(0, SLAB)
    def _(i):
        block = src[i]
        c_src[i] = directed(block)
        s_out[i] = jnp.zeros((PORTS, FIL), f32)
        turned = block[0:8].T
        for place_of, row in enumerate((0, 1, 2, 6)):
            column = turned[:, row : row + 1]
            if row == 6:
                column = column * column
            cols[i, place_of] = jnp.broadcast_to(column, (FIL, 128))

    @pl.loop(0, WINDOW)
    def _(j):
        c_par[j] = directed(par[j])
        p_out[j] = jnp.zeros((PORTS, FIL), f32)

    s_out[SLAB] = jnp.zeros((PORTS, FIL), f32)
    p_out[WINDOW] = jnp.zeros((PORTS, FIL), f32)

    def pair(k):
        row, col = k // 32, k & 31
        i, j = li_ref[row, col], lj_ref[row, col]
        return i, jnp.minimum(i, SLAB - 1), jnp.minimum(j, WINDOW), j & (WINDOW - 1)

    def chunks(k, buf):
        _, i, _, j = pair(k)
        geometry = par[j, 0:8, :]

        def chunk(h, r):
            cut = slice(h * 128, h * 128 + 128)
            xb, yb, zb, rb = [jnp.broadcast_to(geometry[q : q + 1, cut], (16, 128)) for q in (0, 1, 2, 6)]
            xa, ya, za, ra = [cols[i, q, r : r + 16, :] for q in range(4)]
            dx, dy, dz = xa - xb, ya - yb, za - zb
            gap = (ra + rb * rb) + dx * dx + dy * dy + dz * dz
            buf[r : r + 16, cut] = lax.rsqrt(gap).astype(bf16)

        return [functools.partial(chunk, h, r) for h in range(2) for r in range(0, FIL, 16)]

    def fold(product, dirs):
        both = product[0 : 3 * PORTS] + product[3 * PORTS : 6 * PORTS]
        return (
            both[0:PORTS] * dirs[0:1] + both[PORTS : 2 * PORTS] * dirs[1:2]
        ) + both[2 * PORTS : 3 * PORTS] * dirs[2:3]

    def step(k_next, buf_next, k, buf):
        work = chunks(k_next, buf_next)
        i_put, i, j_put, j = pair(k)
        behind = lax.dot_general(c_src[i], buf[...], (((1,), (0,)), ((), ())), preferred_element_type=f32)
        for piece in work[:16]:
            piece()
        p_out[j_put] += fold(behind, par[j, 3:6, :])
        ahead = lax.dot_general(c_par[j], buf[...], (((1,), (1,)), ((), ())), preferred_element_type=f32)
        for piece in work[16:]:
            piece()
        s_out[i_put] += fold(ahead, src[i, 3:6, :])

    for piece in chunks(0, even):
        piece()

    @pl.loop(0, (n + UNROLL - 1) // UNROLL)
    def _(turn):
        k = UNROLL * turn
        for q in range(UNROLL):
            now, later = (even, odd) if q % 2 == 0 else (odd, even)
            step(k + q + 1, later, k + q, now)


def tiles(n, li, lj, src, par):
    sm = pl.BlockSpec(memory_space=pltpu.SMEM)
    vm = pl.BlockSpec(memory_space=pltpu.VMEM)
    return pl.pallas_call(
        tiles_kernel,
        out_shape=[
            jax.ShapeDtypeStruct((SLAB + 1, PORTS, FIL), f32),
            jax.ShapeDtypeStruct((WINDOW + 1, PORTS, FIL), f32),
        ],
        in_specs=[sm, sm, sm, vm, vm],
        out_specs=[vm, vm],
        scratch_shapes=[
            pltpu.VMEM((SLAB, 6 * PORTS, FIL), bf16),
            pltpu.VMEM((WINDOW, 6 * PORTS, FIL), bf16),
            pltpu.VMEM((SLAB, 4, FIL, 128), f32),
            pltpu.VMEM((FIL, FIL), bf16),
            pltpu.VMEM((FIL, FIL), bf16),
        ],
        compiler_params=pltpu.CompilerParams(vmem_limit_bytes=56 * 2**20),
    )(n, li, lj, src, par)


def return_kernel(
    s_part, p_part, out, x_buf, y_buf, z_buf, z_out, y_send, y_recv, z_send, z_recv, c_send, c_recv
):
    wide, member, core, twin, ahead, behind = place()
    mates = [lax.rem(member + step, MEMBERS) for step in range(1, MEMBERS)]
    greet([(wide, mate) for mate in mates] + [(behind, member), (twin, member)])
    half = BLK // PARTS
    core_copies = {}
    for hop in range(HOPS - 1, -1, -1):
        for part in range(PARTS):
            copy = remote(
                p_part.at[pl.ds((2 * hop + 1 - core) * BLK + part * half, half)],
                x_buf.at[hop, pl.ds(part * half, half)],
                c_send.at[hop, part], c_recv.at[hop, part], (twin, member),
            )
            copy.start()
            core_copies[hop, part] = copy
    unit_copies = []
    for step, mate in enumerate(mates):
        copy = remote(
            s_part.at[pl.ds(mate * BLK, BLK)], y_buf.at[step], y_send.at[step], y_recv.at[step], (wide, mate)
        )
        copy.start()
        unit_copies.append(copy)
    hops = {}
    for hop in range(HOPS - 1, -1, -1):
        for part in range(PARTS):
            cut = pl.ds(part * half, half)
            core_copies[hop, part].wait_recv()
            value = p_part[pl.ds((2 * hop + core) * BLK + part * half, half)] + x_buf[hop, cut]
            if hop < HOPS - 1:
                hops[hop + 1, part].wait_recv()
                value = value + z_buf[hop, cut]
            if hop > 0:
                z_out[hop - 1, cut] = value
                copy = remote(
                    z_out.at[hop - 1, cut], z_buf.at[hop - 1, cut],
                    z_send.at[hop - 1, part], z_recv.at[hop - 1, part], (ahead, member),
                )
                copy.start()
                hops[hop, part] = copy
            else:
                if part == 0:
                    for copy in unit_copies:
                        copy.wait_recv()
                value = value + s_part[pl.ds(member * BLK + part * half, half)]
                for step in range(MEMBERS - 1):
                    value = value + y_buf[step, cut]
                for b in range(half):
                    at = (part * half + b) * FIL
                    out[:, at : at + FIL] = value[b]
    for copy in list(core_copies.values()) + unit_copies + list(hops.values()):
        copy.wait_send()


def send_home(s_part, p_part):
    vm = pl.BlockSpec(memory_space=pltpu.VMEM)
    dma = pltpu.SemaphoreType.DMA
    return pl.pallas_call(
        return_kernel,
        out_shape=jax.ShapeDtypeStruct((PORTS, BLK * FIL), f32),
        in_specs=[vm, vm],
        out_specs=vm,
        scratch_shapes=[
            pltpu.VMEM((HOPS, BLK, PORTS, FIL), f32),
            pltpu.VMEM((MEMBERS - 1, BLK, PORTS, FIL), f32),
            pltpu.VMEM((HOPS - 1, BLK, PORTS, FIL), f32),
            pltpu.VMEM((HOPS - 1, BLK, PORTS, FIL), f32),
            dma((3,)), dma((3,)),
            dma((HOPS - 1, PARTS)), dma((HOPS - 1, PARTS)),
            dma((HOPS, PARTS)), dma((HOPS, PARTS)),
        ],
        compiler_params=pltpu.CompilerParams(
            collective_id=1, has_side_effects=True, vmem_limit_bytes=32 * 2**20
        ),
    )(s_part, p_part)


def on_device(positions, directions, radius, currents, pair_target, pair_count):
    slots = jnp.arange(MAXP, dtype=jnp.int32)
    pairs = jnp.where(slots[None, :] < pair_count[:, None], pair_target, -1).reshape(1, BLK * MAXP)
    src, par, li, lj, n = fetch(positions, directions, radius.reshape(1, BLK * FIL), currents, pairs)
    s_part, p_part = tiles(n, li, lj, src, par)
    return send_home(s_part, p_part)


def solution(mesh):
    return jax.shard_map(
        on_device,
        mesh=mesh,
        in_specs=(
            P(None, ("wide", "narrow")),
            P(None, ("wide", "narrow")),
            P(("wide", "narrow")),
            P(None, ("wide", "narrow")),
            P(("wide", "narrow"), None),
            P(("wide", "narrow")),
        ),
        out_specs=P(None, ("wide", "narrow")),
        check_vma=False,
    )
```

```python
import functools

import jax
import jax.numpy as jnp
from jax import lax
from jax.experimental import pallas as pl
from jax.experimental.pallas import tpu as pltpu
from jax.sharding import PartitionSpec as P

FIL = 256
PORTS = 16
BLK = 8
MAXP = 32
SLAB = 32
MEMBERS = 4
HOPS = 4
ROWS = 24
WINDOW = 2 * HOPS * BLK
LIST = 40 * 32
UNROLL = 8
PARTS = 4
TILES_VMEM = 4 * 2**20
f32 = jnp.float32
bf16 = jnp.bfloat16
MESH = pl.DeviceIdType.MESH


def place():
    wide = lax.axis_index("wide")
    member = lax.axis_index("narrow")
    count = lax.axis_size("wide")
    core = lax.rem(wide, 2)
    twin = wide + 1 - 2 * core
    ahead = lax.rem(wide + 2, count)
    behind = lax.rem(wide + count - 2, count)
    return wide, member, core, twin, ahead, behind


def greet(devices):
    barrier = pltpu.get_barrier_semaphore()
    for device in devices:
        pl.semaphore_signal(barrier, inc=1, device_id=device, device_id_type=MESH)
    pl.semaphore_wait(barrier, len(devices))


def remote(src, dst, send, recv, device):
    return pltpu.make_async_remote_copy(
        src_ref=src, dst_ref=dst, send_sem=send, recv_sem=recv, device_id=device, device_id_type=MESH
    )


def list_pairs(rows, member, core):
    lane = lax.broadcasted_iota(jnp.int32, (8, FIL), 1)
    row = lax.broadcasted_iota(jnp.int32, (8, FIL), 0)
    mine = (rows >= 0) & ((rows & 31) // BLK == member)
    hit = mine.astype(bf16)
    upper = (
        lax.broadcasted_iota(jnp.int32, (FIL, FIL), 0) <= lax.broadcasted_iota(jnp.int32, (FIL, FIL), 1)
    ).astype(bf16)
    inclusive = jnp.dot(hit, upper, preferred_element_type=f32).astype(jnp.int32)
    totals = jnp.sum(mine.astype(jnp.int32), axis=1, keepdims=True)
    base = jnp.full((8, 1), BLK, jnp.int32)
    which = lax.broadcasted_iota(jnp.int32, (8, 1), 0)
    for m in range(MEMBERS - 1):
        base = base + jnp.where(which > m, totals[m : m + 1], 0)
    spot = jnp.where(mine, base + inclusive - 1, -1)
    source = row * BLK + lane // MAXP
    partner = (core + rows // SLAB) * BLK + (rows & 7)
    high = jnp.where(mine, spot // 32, -1)
    low = jnp.where(mine, spot & 31, -1)
    out_i = jnp.zeros((40, 32), f32)
    out_j = jnp.zeros((40, 32), f32)
    spots_high = lax.broadcasted_iota(jnp.int32, (40, FIL), 0)
    spots_low = lax.broadcasted_iota(jnp.int32, (32, FIL), 0)
    contract = (((1,), (1,)), ((), ()))
    for m in range(MEMBERS):
        pick_high = spots_high == high[m : m + 1]
        pick_low = (spots_low == low[m : m + 1]).astype(f32).astype(bf16)
        put_i = jnp.where(pick_high, source[m : m + 1].astype(f32), 0.0).astype(bf16)
        put_j = jnp.where(pick_high, partner[m : m + 1].astype(f32), 0.0).astype(bf16)
        out_i = out_i + lax.dot_general(put_i, pick_low, contract, preferred_element_type=f32)
        out_j = out_j + lax.dot_general(put_j, pick_low, contract, preferred_element_type=f32)
    total = BLK + jnp.sum(totals[0:MEMBERS], axis=0, keepdims=True)
    flat = 32 * lax.broadcasted_iota(jnp.int32, (40, 32), 0) + lax.broadcasted_iota(jnp.int32, (40, 32), 1)
    diagonal = flat < BLK
    used = flat < total
    li = jnp.where(diagonal, member * BLK + flat, jnp.where(used, out_i.astype(jnp.int32), SLAB))
    lj = jnp.where(diagonal, 2 * WINDOW + core * BLK + flat, jnp.where(used, out_j.astype(jnp.int32), WINDOW))
    return li, lj, total


def directed(block):
    cur = block[8:ROWS]
    parts = jnp.concatenate([block[3 + comp : 4 + comp] * cur for comp in range(3)], axis=0)
    head = parts.astype(bf16)
    tail = (parts - head.astype(f32)).astype(bf16)
    return jnp.concatenate([head, tail], axis=0)


def columns(block, spread):
    geometry = jnp.concatenate([block[0:3], block[6:7] * block[6:7]], axis=0)
    head = geometry.astype(bf16).astype(f32)
    rest = geometry - head
    middle = rest.astype(bf16).astype(f32)
    tail = rest - middle
    terms = jnp.concatenate([head, middle, tail, jnp.zeros((4, FIL), f32)], axis=0)
    return jnp.dot(terms.T.astype(bf16), spread, preferred_element_type=f32)


def fetch_kernel(
    packed, pairs,
    src, par, c_src, c_par, cols, table,
    lists, y_send, y_recv, l_send, l_recv, z_send, z_recv, c_send, c_recv,
):
    wide, member, core, twin, ahead, behind = place()
    mates = [lax.rem(member + step, MEMBERS) for step in range(1, MEMBERS)]
    lists[...] = jnp.full((8, FIL), -1, jnp.int32)
    lists[pl.ds(member, 1)] = pairs[...]
    for b in range(BLK):
        block = packed[:, b * FIL : (b + 1) * FIL]
        src[member * BLK + b] = block
        par[core * BLK + b] = block
    greet([(wide, mate) for mate in mates] + [(ahead, member), (twin, member)])
    half = BLK // PARTS
    own = src.at[pl.ds(member * BLK, BLK)]

    def seat(hop, part):
        return pl.ds((2 * hop + core) * BLK + part * half, half)

    hops = [[]]
    for part in range(PARTS):
        copy = remote(
            src.at[pl.ds(member * BLK + part * half, half)], par.at[seat(1, part)],
            z_send.at[0, part], z_recv.at[0, part], (behind, member),
        )
        copy.start()
        hops[0].append(copy)
    list_copies = []
    for step, mate in enumerate(mates):
        row = lists.at[pl.ds(member, 1)]
        copy = remote(row, row, l_send.at[step], l_recv.at[step], (wide, mate))
        copy.start()
        list_copies.append(copy)
    unit_copies = []
    for step, mate in enumerate(mates):
        copy = remote(own, own, y_send.at[step], y_recv.at[step], (wide, mate))
        copy.start()
        unit_copies.append(copy)
    core_copies = {}
    copy = remote(own, par.at[pl.ds(core * BLK, BLK)], c_send.at[0, 0], c_recv.at[0, 0], (twin, member))
    copy.start()
    core_copies[0, 0] = copy

    term = lax.broadcasted_iota(jnp.int32, (16, 512), 0)
    group = lax.broadcasted_iota(jnp.int32, (16, 512), 1) // 128
    spread = jnp.where((term < 12) & (lax.rem(term, 4) == group), 1.0, 0.0).astype(bf16)

    def ready_sources(first):
        @pl.loop(0, BLK // 4)
        def _(quad):
            for b in range(4):
                i = first + 4 * quad + b
                block = src[i]
                c_src[i] = directed(block)
                wide_columns = columns(block, spread)
                for q in range(4):
                    cols[i, q] = wide_columns[:, q * 128 : (q + 1) * 128]

    def ready_partners(first, count_of):
        @pl.loop(0, count_of // 2)
        def _(duo):
            for b in range(2):
                j = first + 2 * duo + b
                c_par[j] = directed(par[j])

    def pass_on(hop):
        later = []
        for part in range(PARTS):
            hops[hop - 1][part].wait_recv()
            if hop < HOPS - 1:
                copy = remote(
                    par.at[seat(hop, part)], par.at[seat(hop + 1, part)],
                    z_send.at[hop, part], z_recv.at[hop, part], (behind, member),
                )
                copy.start()
                later.append(copy)
            copy = remote(
                par.at[seat(hop, part)], par.at[seat(hop, part)],
                c_send.at[hop, part], c_recv.at[hop, part], (twin, member),
            )
            copy.start()
            core_copies[hop, part] = copy
        hops.append(later)

    def from_core(hop):
        for part in range(PARTS if hop else 1):
            core_copies[hop, part].wait_recv()

    def mate_of(step):
        return lax.rem(member + MEMBERS - 1 - step, MEMBERS)

    ready_sources(member * BLK)
    for copy in list_copies:
        copy.wait()
    li, lj, total = list_pairs(lists[...], member, core)
    table[0:40] = li
    table[40:80] = lj
    table[80:88] = jnp.broadcast_to(total, (8, 32))
    pass_on(1)
    for step in (0, 2):
        unit_copies[step].wait_recv()
        ready_sources(mate_of(step) * BLK)
    pass_on(2)
    unit_copies[1].wait_recv()
    ready_sources(mate_of(1) * BLK)
    from_core(0)
    ready_partners(0, 2 * BLK)
    from_core(1)
    ready_partners(2 * BLK, 2 * BLK)
    pass_on(3)
    from_core(2)
    ready_partners(4 * BLK, 2 * BLK)
    ready_partners((6 + core) * BLK, BLK)
    from_core(3)
    ready_partners((7 - core) * BLK, BLK)
    for group_of in hops:
        for copy in group_of:
            copy.wait_send()
    for copy in unit_copies + list(core_copies.values()):
        copy.wait_send()


def fetch(packed, pairs):
    vm = pl.BlockSpec(memory_space=pltpu.VMEM)
    dma = pltpu.SemaphoreType.DMA
    return pl.pallas_call(
        fetch_kernel,
        out_shape=[
            jax.ShapeDtypeStruct((SLAB, ROWS, FIL), f32),
            jax.ShapeDtypeStruct((WINDOW, ROWS, FIL), f32),
            jax.ShapeDtypeStruct((SLAB, 6 * PORTS, FIL), bf16),
            jax.ShapeDtypeStruct((WINDOW, 6 * PORTS, FIL), bf16),
            jax.ShapeDtypeStruct((SLAB, 4, FIL, 128), f32),
            jax.ShapeDtypeStruct((88, 32), jnp.int32),
        ],
        in_specs=[vm] * 2,
        out_specs=[vm] * 6,
        scratch_shapes=[
            pltpu.VMEM((8, FIL), jnp.int32),
            dma((3,)), dma((3,)), dma((3,)), dma((3,)),
            dma((3, PARTS)), dma((3, PARTS)),
            dma((HOPS, PARTS)), dma((HOPS, PARTS)),
        ],
        compiler_params=pltpu.CompilerParams(
            collective_id=0, has_side_effects=True, vmem_limit_bytes=8 * 2**20
        ),
    )(packed, pairs)


def tiles_kernel(table, src, par, c_src, c_par, cols, s_out, p_out, even, odd, turns, sem):
    load = pltpu.make_async_copy(table, turns, sem)
    load.start()

    @pl.loop(0, SLAB + 1)
    def _(i):
        s_out[i] = jnp.zeros((PORTS, FIL), f32)

    @pl.loop(0, WINDOW + 1)
    def _(j):
        p_out[j] = jnp.zeros((PORTS, FIL), f32)

    load.wait()
    n = turns[80, 0]

    def pair(k):
        row, col = k // 32, k & 31
        i, j = turns[row, col], turns[40 + row, col]
        return i, jnp.minimum(i, SLAB - 1), jnp.minimum(j, WINDOW), j & (WINDOW - 1)

    def chunks(k, buf):
        _, i, _, j = pair(k)
        geometry = par[j, 0:8, :]

        def chunk(h, r):
            cut = slice(h * 128, h * 128 + 128)
            xb, yb, zb, rb = [jnp.broadcast_to(geometry[q : q + 1, cut], (16, 128)) for q in (0, 1, 2, 6)]
            xa, ya, za, ra = [cols[i, q, r : r + 16, :] for q in range(4)]
            dx, dy, dz = xa - xb, ya - yb, za - zb
            gap = (ra + rb * rb) + dx * dx + dy * dy + dz * dz
            buf[r : r + 16, cut] = lax.rsqrt(gap).astype(bf16)

        return [functools.partial(chunk, h, r) for h in range(2) for r in range(0, FIL, 16)]

    def fold(product, dirs):
        both = product[0 : 3 * PORTS] + product[3 * PORTS : 6 * PORTS]
        return (
            both[0:PORTS] * dirs[0:1] + both[PORTS : 2 * PORTS] * dirs[1:2]
        ) + both[2 * PORTS : 3 * PORTS] * dirs[2:3]

    def step(k_next, buf_next, k, buf):
        work = chunks(k_next, buf_next)
        i_put, i, j_put, j = pair(k)
        behind = lax.dot_general(c_src[i], buf[...], (((1,), (0,)), ((), ())), preferred_element_type=f32)
        for piece in work[:16]:
            piece()
        p_out[j_put] += fold(behind, par[j, 3:6, :])
        ahead = lax.dot_general(c_par[j], buf[...], (((1,), (1,)), ((), ())), preferred_element_type=f32)
        for piece in work[16:]:
            piece()
        s_out[i_put] += fold(ahead, src[i, 3:6, :])

    for piece in chunks(0, even):
        piece()

    @pl.loop(0, (n + UNROLL - 1) // UNROLL)
    def _(turn):
        k = UNROLL * turn
        for q in range(UNROLL):
            now, later = (even, odd) if q % 2 == 0 else (odd, even)
            step(k + q + 1, later, k + q, now)


def tiles(table, src, par, c_src, c_par, cols):
    vm = pl.BlockSpec(memory_space=pltpu.VMEM)
    return pl.pallas_call(
        tiles_kernel,
        out_shape=[
            jax.ShapeDtypeStruct((SLAB + 1, PORTS, FIL), f32),
            jax.ShapeDtypeStruct((WINDOW + 1, PORTS, FIL), f32),
        ],
        in_specs=[vm] * 6,
        out_specs=[vm] * 2,
        scratch_shapes=[
            pltpu.VMEM((FIL, FIL), bf16),
            pltpu.VMEM((FIL, FIL), bf16),
            pltpu.SMEM((88, 32), jnp.int32),
            pltpu.SemaphoreType.DMA,
        ],
        compiler_params=pltpu.CompilerParams(vmem_limit_bytes=TILES_VMEM),
    )(table, src, par, c_src, c_par, cols)


def return_kernel(
    s_part, p_part, out, x_buf, y_buf, z_buf, z_out, y_send, y_recv, z_send, z_recv, c_send, c_recv
):
    wide, member, core, twin, ahead, behind = place()
    mates = [lax.rem(member + step, MEMBERS) for step in range(1, MEMBERS)]
    greet([(wide, mate) for mate in mates] + [(behind, member), (twin, member)])
    half = BLK // PARTS
    core_copies = {}
    for hop in range(HOPS - 1, -1, -1):
        for part in range(PARTS):
            copy = remote(
                p_part.at[pl.ds((2 * hop + 1 - core) * BLK + part * half, half)],
                x_buf.at[hop, pl.ds(part * half, half)],
                c_send.at[hop, part], c_recv.at[hop, part], (twin, member),
            )
            copy.start()
            core_copies[hop, part] = copy
    unit_copies = []
    for step, mate in enumerate(mates):
        copy = remote(
            s_part.at[pl.ds(mate * BLK, BLK)], y_buf.at[step], y_send.at[step], y_recv.at[step], (wide, mate)
        )
        copy.start()
        unit_copies.append(copy)
    hops = {}
    for hop in range(HOPS - 1, -1, -1):
        for part in range(PARTS):
            cut = pl.ds(part * half, half)
            core_copies[hop, part].wait_recv()
            value = p_part[pl.ds((2 * hop + core) * BLK + part * half, half)] + x_buf[hop, cut]
            if hop < HOPS - 1:
                hops[hop + 1, part].wait_recv()
                value = value + z_buf[hop, cut]
            if hop > 0:
                z_out[hop - 1, cut] = value
                copy = remote(
                    z_out.at[hop - 1, cut], z_buf.at[hop - 1, cut],
                    z_send.at[hop - 1, part], z_recv.at[hop - 1, part], (ahead, member),
                )
                copy.start()
                hops[hop, part] = copy
            else:
                if part == 0:
                    for copy in unit_copies:
                        copy.wait_recv()
                value = value + s_part[pl.ds(member * BLK + part * half, half)]
                for step in range(MEMBERS - 1):
                    value = value + y_buf[step, cut]
                for b in range(half):
                    at = (part * half + b) * FIL
                    out[:, at : at + FIL] = value[b]
    for copy in list(core_copies.values()) + unit_copies + list(hops.values()):
        copy.wait_send()


def send_home(s_part, p_part):
    vm = pl.BlockSpec(memory_space=pltpu.VMEM)
    dma = pltpu.SemaphoreType.DMA
    return pl.pallas_call(
        return_kernel,
        out_shape=jax.ShapeDtypeStruct((PORTS, BLK * FIL), f32),
        in_specs=[vm, vm],
        out_specs=vm,
        scratch_shapes=[
            pltpu.VMEM((HOPS, BLK, PORTS, FIL), f32),
            pltpu.VMEM((MEMBERS - 1, BLK, PORTS, FIL), f32),
            pltpu.VMEM((HOPS - 1, BLK, PORTS, FIL), f32),
            pltpu.VMEM((HOPS - 1, BLK, PORTS, FIL), f32),
            dma((3,)), dma((3,)),
            dma((HOPS - 1, PARTS)), dma((HOPS - 1, PARTS)),
            dma((HOPS, PARTS)), dma((HOPS, PARTS)),
        ],
        compiler_params=pltpu.CompilerParams(
            collective_id=1, has_side_effects=True, vmem_limit_bytes=8 * 2**20
        ),
    )(s_part, p_part)


def on_device(positions, directions, radius, currents, pair_target, pair_count):
    rad = radius.reshape(1, BLK * FIL)
    packed = jnp.concatenate([positions, directions, rad, rad, currents], axis=0)
    slots = jnp.arange(MAXP, dtype=jnp.int32)
    pairs = jnp.where(slots[None, :] < pair_count[:, None], pair_target, -1).reshape(1, BLK * MAXP)
    fetched = fetch(packed, pairs)
    src, par, c_src, c_par, cols, table = fetched
    s_part, p_part = tiles(table, src, par, c_src, c_par, cols)
    return send_home(s_part, p_part)


def solution(mesh):
    return jax.shard_map(
        on_device,
        mesh=mesh,
        in_specs=(
            P(None, ("wide", "narrow")),
            P(None, ("wide", "narrow")),
            P(("wide", "narrow")),
            P(None, ("wide", "narrow")),
            P(("wide", "narrow"), None),
            P(("wide", "narrow")),
        ),
        out_specs=P(None, ("wide", "narrow")),
        check_vma=False,
    )
```

```python
import functools

import jax
import jax.numpy as jnp
from jax import lax
from jax.experimental import pallas as pl
from jax.experimental.pallas import tpu as pltpu
from jax.sharding import PartitionSpec as P

FIL = 256
PORTS = 16
BLK = 8
MAXP = 32
SLAB = 32
MEMBERS = 4
HOPS = 4
ROWS = 24
WINDOW = 2 * HOPS * BLK
ALL = SLAB + WINDOW
LIST = 40
UNROLL = 8
PARTS = 4
TILES_VMEM = 4 * 2**20
f32 = jnp.float32
bf16 = jnp.bfloat16
MESH = pl.DeviceIdType.MESH


def place():
    wide = lax.axis_index("wide")
    member = lax.axis_index("narrow")
    count = lax.axis_size("wide")
    core = lax.rem(wide, 2)
    twin = wide + 1 - 2 * core
    ahead = lax.rem(wide + 2, count)
    behind = lax.rem(wide + count - 2, count)
    return wide, member, core, twin, ahead, behind


def greet(devices):
    barrier = pltpu.get_barrier_semaphore()
    for device in devices:
        pl.semaphore_signal(barrier, inc=1, device_id=device, device_id_type=MESH)
    pl.semaphore_wait(barrier, len(devices))


def remote(src, dst, send, recv, device):
    return pltpu.make_async_remote_copy(
        src_ref=src, dst_ref=dst, send_sem=send, recv_sem=recv, device_id=device, device_id_type=MESH
    )


def list_pairs(rows, member, core):
    lane = lax.broadcasted_iota(jnp.int32, (8, FIL), 1)
    row = lax.broadcasted_iota(jnp.int32, (8, FIL), 0)
    which = lax.broadcasted_iota(jnp.int32, (8, 1), 0)
    home = which < MEMBERS
    upper = (
        lax.broadcasted_iota(jnp.int32, (FIL, FIL), 0) <= lax.broadcasted_iota(jnp.int32, (FIL, FIL), 1)
    ).astype(bf16)

    def by_row(chosen):
        return jnp.sum(chosen.astype(jnp.int32), axis=1, keepdims=True)

    def by_slab(chosen):
        counts = by_row(chosen)
        own = jnp.sum(jnp.where(home, counts, 0), axis=0, keepdims=True)
        twin = jnp.sum(jnp.where(home, 0, counts), axis=0, keepdims=True)
        return own, twin

    def rank(chosen, apart):
        inclusive = jnp.dot(chosen.astype(f32).astype(bf16), upper, preferred_element_type=f32)
        counts = by_row(chosen)
        base = jnp.zeros((8, 1), jnp.int32)
        for m in range(7):
            later = which > m
            if apart:
                later = later & (home == (m < MEMBERS))
            base = base + jnp.where(later, counts[m : m + 1], 0)
        return base + inclusive.astype(jnp.int32) - 1

    valid = rows >= 0
    offset = rows // SLAB
    quarter = (rows & (SLAB - 1)) // BLK
    source = (row & (MEMBERS - 1)) * BLK + lane // MAXP
    free = valid & (offset == 0)
    fixed = valid & (offset > 0)
    shares = [by_slab(fixed & (quarter == q)) for q in range(MEMBERS)]
    free_total = by_slab(free)
    begin, width = [], []
    for slab in range(2):
        known = [share[slab] for share in shares]
        level = (known[0] + known[1] + known[2] + known[3] + free_total[slab] + MEMBERS - 1) // MEMBERS
        room = [jnp.maximum(level - share, 0) for share in known]
        first = jnp.zeros((1, 1), jnp.int32)
        span = jnp.zeros((1, 1), jnp.int32)
        for q in range(MEMBERS):
            first = first + jnp.where(member > q, room[q], 0)
            span = span + jnp.where(member == q, room[q], 0)
        begin.append(first)
        width.append(span)
    begins = jnp.where(home, begin[0], begin[1])
    ends = begins + jnp.where(home, width[0], width[1])
    free_rank = rank(free, True)
    dealt = (fixed & (quarter == member)) | (free & (free_rank >= begins) & (free_rank < ends))
    loads = by_slab(dealt)
    movable = dealt & (quarter == member) & (source // BLK == member)
    movable_rank = rank(movable, True)
    give = jnp.maximum(loads[0] - loads[1], 0) // 2
    take = jnp.maximum(loads[1] - loads[0], 0) // 2
    crosses = movable & (movable_rank < jnp.where(home, give, take))
    mine = (dealt & home & ~crosses) | (crosses & ~home)
    spot = rank(mine, False)
    total = jnp.sum(by_row(mine), axis=0, keepdims=True)
    there = jnp.where(home, core, 1 - core)
    in_window = SLAB + (there + offset) * BLK + (rows & (BLK - 1))
    partner = jnp.where(home & (offset == 0), rows & (SLAB - 1), in_window)
    source = jnp.where(home, source, SLAB + there * BLK + (source & (BLK - 1)))
    high = jnp.where(mine, spot // 32, -1)
    low = jnp.where(mine, spot & 31, -1)
    out_i = jnp.zeros((LIST, 32), f32)
    out_j = jnp.zeros((LIST, 32), f32)
    spots_high = lax.broadcasted_iota(jnp.int32, (LIST, FIL), 0)
    spots_low = lax.broadcasted_iota(jnp.int32, (32, FIL), 0)
    contract = (((1,), (1,)), ((), ()))
    for m in range(8):
        pick_high = spots_high == high[m : m + 1]
        pick_low = (spots_low == low[m : m + 1]).astype(f32).astype(bf16)
        put_i = jnp.where(pick_high, source[m : m + 1].astype(f32), 0.0).astype(bf16)
        put_j = jnp.where(pick_high, partner[m : m + 1].astype(f32), 0.0).astype(bf16)
        out_i = out_i + lax.dot_general(put_i, pick_low, contract, preferred_element_type=f32)
        out_j = out_j + lax.dot_general(put_j, pick_low, contract, preferred_element_type=f32)
    flat = 32 * lax.broadcasted_iota(jnp.int32, (LIST, 32), 0) + lax.broadcasted_iota(jnp.int32, (LIST, 32), 1)
    used = flat < total
    li = jnp.where(used, out_i.astype(jnp.int32), ALL)
    lj = jnp.where(used, out_j.astype(jnp.int32), ALL)
    return li, lj, total


def directed(block):
    cur = block[8:ROWS]
    parts = jnp.concatenate([block[3 + comp : 4 + comp] * cur for comp in range(3)], axis=0)
    head = parts.astype(bf16)
    tail = (parts - head.astype(f32)).astype(bf16)
    return jnp.concatenate([head, tail], axis=0)


def columns(block, spread):
    geometry = jnp.concatenate([block[0:3], block[6:7] * block[6:7]], axis=0)
    head = geometry.astype(bf16).astype(f32)
    rest = geometry - head
    middle = rest.astype(bf16).astype(f32)
    tail = rest - middle
    terms = jnp.concatenate([head, middle, tail, jnp.zeros((4, FIL), f32)], axis=0)
    return jnp.dot(terms.T.astype(bf16), spread, preferred_element_type=f32)


def tile_pieces(cols, i, geometry, buf):
    radius = geometry[6:7] * geometry[6:7]

    def piece(h, r):
        cut = slice(h * 128, h * 128 + 128)
        xb, yb, zb = [jnp.broadcast_to(geometry[q : q + 1, cut], (16, 128)) for q in range(3)]
        rb = jnp.broadcast_to(radius[:, cut], (16, 128))
        xa, ya, za, ra = [cols[i, q, r : r + 16, :] for q in range(4)]
        dx, dy, dz = xa - xb, ya - yb, za - zb
        gap = (ra + rb) + dx * dx + dy * dy + dz * dz
        buf[r : r + 16, cut] = lax.rsqrt(gap).astype(bf16)

    return [functools.partial(piece, h, r) for h in range(2) for r in range(0, FIL, 16)]


def fold(product, dirs):
    both = product[0 : 3 * PORTS] + product[3 * PORTS : 6 * PORTS]
    return (
        both[0:PORTS] * dirs[0:1] + both[PORTS : 2 * PORTS] * dirs[1:2]
    ) + both[2 * PORTS : 3 * PORTS] * dirs[2:3]


def fetch_kernel(
    packed, pairs,
    blocks, terms, cols, acc, table,
    lists, tile, t_send, t_recv, y_send, y_recv, l_send, l_recv, z_send, z_recv, c_send, c_recv,
):
    wide, member, core, twin, ahead, behind = place()
    mates = [lax.rem(member + step, MEMBERS) for step in range(1, MEMBERS)]
    lists[...] = jnp.full((8, FIL), -1, jnp.int32)
    lists[pl.ds(member, 1)] = pairs[...]
    for b in range(BLK):
        block = packed[:, b * FIL : (b + 1) * FIL]
        blocks[member * BLK + b] = block
        blocks[SLAB + core * BLK + b] = block
    greet([(wide, mate) for mate in mates] + [(ahead, member), (twin, member)])
    half = BLK // PARTS
    own = blocks.at[pl.ds(member * BLK, BLK)]

    def seat(hop, part):
        return pl.ds(SLAB + (2 * hop + core) * BLK + part * half, half)

    hops = [[]]
    for part in range(PARTS):
        copy = remote(
            blocks.at[pl.ds(member * BLK + part * half, half)], blocks.at[seat(1, part)],
            z_send.at[0, part], z_recv.at[0, part], (behind, member),
        )
        copy.start()
        hops[0].append(copy)
    list_copies = []
    for step, mate in enumerate(mates):
        row = lists.at[pl.ds(member, 1)]
        copy = remote(row, row, l_send.at[step], l_recv.at[step], (wide, mate))
        copy.start()
        list_copies.append(copy)
    unit_copies = []
    for step, mate in enumerate(mates):
        copy = remote(own, own, y_send.at[step], y_recv.at[step], (wide, mate))
        copy.start()
        unit_copies.append(copy)
    core_copies = {}
    copy = remote(own, blocks.at[pl.ds(SLAB + core * BLK, BLK)], c_send.at[0, 0], c_recv.at[0, 0], (twin, member))
    copy.start()
    core_copies[0, 0] = copy

    term = lax.broadcasted_iota(jnp.int32, (16, 512), 0)
    group = lax.broadcasted_iota(jnp.int32, (16, 512), 1) // 128
    spread = jnp.where((term < 12) & (lax.rem(term, 4) == group), 1.0, 0.0).astype(bf16)

    def ready_sources(first, held):
        @pl.loop(0, BLK // 4)
        def _(quad):
            for b in range(4):
                i = first + 4 * quad + b
                block = blocks[i]
                terms[i] = directed(block)
                wide_columns = columns(block, spread)
                for q in range(4):
                    cols[held + 4 * quad + b, q] = wide_columns[:, q * 128 : (q + 1) * 128]

    def ready_partners(first, count_of):
        @pl.loop(0, count_of // 2)
        def _(duo):
            for b in range(2):
                j = SLAB + first + 2 * duo + b
                terms[j] = directed(blocks[j])

    def pass_on(hop):
        later = []
        for part in range(PARTS):
            hops[hop - 1][part].wait_recv()
            if hop < HOPS - 1:
                copy = remote(
                    blocks.at[seat(hop, part)], blocks.at[seat(hop + 1, part)],
                    z_send.at[hop, part], z_recv.at[hop, part], (behind, member),
                )
                copy.start()
                later.append(copy)
            copy = remote(
                blocks.at[seat(hop, part)], blocks.at[seat(hop, part)],
                c_send.at[hop, part], c_recv.at[hop, part], (twin, member),
            )
            copy.start()
            core_copies[hop, part] = copy
        hops.append(later)

    def from_core(hop):
        for part in range(PARTS if hop else 1):
            core_copies[hop, part].wait_recv()

    def mate_of(step):
        return lax.rem(member + MEMBERS - 1 - step, MEMBERS)

    @pl.loop(0, ALL + 1)
    def _(i):
        acc[i] = jnp.zeros((PORTS, FIL), f32)

    ready_sources(member * BLK, member * BLK)
    for copy in list_copies:
        copy.wait()
    twin_lists = remote(
        lists.at[pl.ds(0, MEMBERS)], lists.at[pl.ds(MEMBERS, MEMBERS)], t_send, t_recv, (twin, member)
    )
    twin_lists.start()
    pass_on(1)
    twin_lists.wait()
    li, lj, total = list_pairs(lists[...], member, core)
    table[0:LIST] = li
    table[LIST : 2 * LIST] = lj
    table[2 * LIST : 2 * LIST + 8] = jnp.broadcast_to(total, (8, 32))
    for step in (0, 2):
        unit_copies[step].wait_recv()
        ready_sources(mate_of(step) * BLK, mate_of(step) * BLK)
    pass_on(2)
    unit_copies[1].wait_recv()
    ready_sources(mate_of(1) * BLK, mate_of(1) * BLK)

    @pl.loop(0, BLK)
    def _(b):
        i = member * BLK + b
        for piece in tile_pieces(cols, i, blocks[i, 0:8, :], tile):
            piece()
        product = lax.dot_general(terms[i], tile[...], (((1,), (1,)), ((), ())), preferred_element_type=f32)
        acc[i] = fold(product, blocks[i, 3:6, :])

    from_core(0)
    ready_sources(SLAB + (1 - core) * BLK, SLAB)
    ready_partners(core * BLK, BLK)
    from_core(1)
    ready_partners(2 * BLK, 2 * BLK)
    pass_on(3)
    from_core(2)
    ready_partners(4 * BLK, 2 * BLK)
    ready_partners((6 + core) * BLK, BLK)
    from_core(3)
    ready_partners((7 - core) * BLK, BLK)
    for group_of in hops:
        for copy in group_of:
            copy.wait_send()
    for copy in unit_copies + list(core_copies.values()):
        copy.wait_send()


def fetch(packed, pairs):
    vm = pl.BlockSpec(memory_space=pltpu.VMEM)
    dma = pltpu.SemaphoreType.DMA
    return pl.pallas_call(
        fetch_kernel,
        out_shape=[
            jax.ShapeDtypeStruct((ALL, ROWS, FIL), f32),
            jax.ShapeDtypeStruct((ALL, 6 * PORTS, FIL), bf16),
            jax.ShapeDtypeStruct((SLAB + BLK, 4, FIL, 128), f32),
            jax.ShapeDtypeStruct((ALL + 1, PORTS, FIL), f32),
            jax.ShapeDtypeStruct((88, 32), jnp.int32),
        ],
        in_specs=[vm] * 2,
        out_specs=[vm] * 5,
        scratch_shapes=[
            pltpu.VMEM((8, FIL), jnp.int32),
            pltpu.VMEM((FIL, FIL), bf16),
            dma, dma,
            dma((3,)), dma((3,)), dma((3,)), dma((3,)),
            dma((3, PARTS)), dma((3, PARTS)),
            dma((HOPS, PARTS)), dma((HOPS, PARTS)),
        ],
        compiler_params=pltpu.CompilerParams(
            collective_id=0, has_side_effects=True, vmem_limit_bytes=8 * 2**20
        ),
    )(packed, pairs)


def tiles_kernel(table, blocks, terms, cols, start, acc, even, odd, turns, sem):
    load = pltpu.make_async_copy(table, turns, sem)
    load.start()
    load.wait()
    n = turns[2 * LIST, 0]

    def pair(k):
        row, col = k // 32, k & 31
        return turns[row, col], turns[LIST + row, col]

    def chunks(k, buf):
        i, j = pair(k)
        held = jnp.where(i < SLAB, i, SLAB + (i & (BLK - 1)))
        return tile_pieces(cols, held, blocks[jnp.minimum(j, ALL - 1), 0:8, :], buf)

    def step(k_next, buf_next, k, buf):
        work = chunks(k_next, buf_next)
        i_put, j_put = pair(k)
        i, j = jnp.minimum(i_put, ALL - 1), jnp.minimum(j_put, ALL - 1)
        behind = lax.dot_general(terms[i], buf[...], (((1,), (0,)), ((), ())), preferred_element_type=f32)
        for piece in work[:16]:
            piece()
        acc[j_put] += fold(behind, blocks[j, 3:6, :])
        ahead = lax.dot_general(terms[j], buf[...], (((1,), (1,)), ((), ())), preferred_element_type=f32)
        for piece in work[16:]:
            piece()
        acc[i_put] += fold(ahead, blocks[i, 3:6, :])

    for piece in chunks(0, even):
        piece()

    @pl.loop(0, (n + UNROLL - 1) // UNROLL)
    def _(turn):
        k = UNROLL * turn
        for q in range(UNROLL):
            now, later = (even, odd) if q % 2 == 0 else (odd, even)
            step(k + q + 1, later, k + q, now)


def tiles(table, blocks, terms, cols, acc):
    vm = pl.BlockSpec(memory_space=pltpu.VMEM)
    return pl.pallas_call(
        tiles_kernel,
        out_shape=jax.ShapeDtypeStruct((ALL + 1, PORTS, FIL), f32),
        in_specs=[vm] * 5,
        out_specs=vm,
        scratch_shapes=[
            pltpu.VMEM((FIL, FIL), bf16),
            pltpu.VMEM((FIL, FIL), bf16),
            pltpu.SMEM((88, 32), jnp.int32),
            pltpu.SemaphoreType.DMA,
        ],
        input_output_aliases={4: 0},
        compiler_params=pltpu.CompilerParams(vmem_limit_bytes=TILES_VMEM),
    )(table, blocks, terms, cols, acc)


def return_kernel(
    acc, out, x_buf, y_buf, z_buf, z_out, y_send, y_recv, z_send, z_recv, c_send, c_recv
):
    wide, member, core, twin, ahead, behind = place()
    mates = [lax.rem(member + step, MEMBERS) for step in range(1, MEMBERS)]
    greet([(wide, mate) for mate in mates] + [(behind, member), (twin, member)])
    half = BLK // PARTS
    core_copies = {}
    for hop in range(HOPS - 1, -1, -1):
        for part in range(PARTS):
            copy = remote(
                acc.at[pl.ds(SLAB + (2 * hop + 1 - core) * BLK + part * half, half)],
                x_buf.at[hop, pl.ds(part * half, half)],
                c_send.at[hop, part], c_recv.at[hop, part], (twin, member),
            )
            copy.start()
            core_copies[hop, part] = copy
    unit_copies = []
    for step, mate in enumerate(mates):
        copy = remote(
            acc.at[pl.ds(mate * BLK, BLK)], y_buf.at[step], y_send.at[step], y_recv.at[step], (wide, mate)
        )
        copy.start()
        unit_copies.append(copy)
    hops = {}
    for hop in range(HOPS - 1, -1, -1):
        for part in range(PARTS):
            cut = pl.ds(part * half, half)
            core_copies[hop, part].wait_recv()
            value = x_buf[hop, cut] + acc[pl.ds(SLAB + (2 * hop + core) * BLK + part * half, half)]
            if hop < HOPS - 1:
                hops[hop + 1, part].wait_recv()
                value = value + z_buf[hop, cut]
            if hop > 0:
                z_out[hop - 1, cut] = value
                copy = remote(
                    z_out.at[hop - 1, cut], z_buf.at[hop - 1, cut],
                    z_send.at[hop - 1, part], z_recv.at[hop - 1, part], (ahead, member),
                )
                copy.start()
                hops[hop, part] = copy
            else:
                if part == 0:
                    for copy in unit_copies:
                        copy.wait_recv()
                value = value + acc[pl.ds(member * BLK + part * half, half)]
                for step in range(MEMBERS - 1):
                    value = value + y_buf[step, cut]
                for b in range(half):
                    at = (part * half + b) * FIL
                    out[:, at : at + FIL] = value[b]
    for copy in list(core_copies.values()) + unit_copies + list(hops.values()):
        copy.wait_send()


def send_home(acc):
    vm = pl.BlockSpec(memory_space=pltpu.VMEM)
    dma = pltpu.SemaphoreType.DMA
    return pl.pallas_call(
        return_kernel,
        out_shape=jax.ShapeDtypeStruct((PORTS, BLK * FIL), f32),
        in_specs=[vm],
        out_specs=vm,
        scratch_shapes=[
            pltpu.VMEM((HOPS, BLK, PORTS, FIL), f32),
            pltpu.VMEM((MEMBERS - 1, BLK, PORTS, FIL), f32),
            pltpu.VMEM((HOPS - 1, BLK, PORTS, FIL), f32),
            pltpu.VMEM((HOPS - 1, BLK, PORTS, FIL), f32),
            dma((3,)), dma((3,)),
            dma((HOPS - 1, PARTS)), dma((HOPS - 1, PARTS)),
            dma((HOPS, PARTS)), dma((HOPS, PARTS)),
        ],
        compiler_params=pltpu.CompilerParams(
            collective_id=1, has_side_effects=True, vmem_limit_bytes=8 * 2**20
        ),
    )(acc)


def on_device(positions, directions, radius, currents, pair_target, pair_count):
    rad = radius.reshape(1, BLK * FIL)
    packed = jnp.concatenate([positions, directions, rad, rad, currents], axis=0)
    slots = jnp.arange(MAXP, dtype=jnp.int32)
    pairs = jnp.where(slots[None, :] < pair_count[:, None], pair_target, -1).reshape(1, BLK * MAXP)
    blocks, terms, cols, acc, table = fetch(packed, pairs)
    return send_home(tiles(table, blocks, terms, cols, acc))


def solution(mesh):
    return jax.shard_map(
        on_device,
        mesh=mesh,
        in_specs=(
            P(None, ("wide", "narrow")),
            P(None, ("wide", "narrow")),
            P(("wide", "narrow")),
            P(None, ("wide", "narrow")),
            P(("wide", "narrow"), None),
            P(("wide", "narrow")),
        ),
        out_specs=P(None, ("wide", "narrow")),
        check_vma=False,
    )
```

```python
import functools

import jax
import jax.numpy as jnp
from jax import lax
from jax.experimental import pallas as pl
from jax.experimental.pallas import tpu as pltpu
from jax.sharding import PartitionSpec as P

FIL = 256
PORTS = 16
BLK = 8
MAXP = 32
SLAB = 32
MEMBERS = 4
HOPS = 4
ROWS = 24
WINDOW = 2 * HOPS * BLK
ALL = SLAB + WINDOW
LIST = 40
UNROLL = 8
PARTS = 4
TILES_VMEM = 4 * 2**20
f32 = jnp.float32
bf16 = jnp.bfloat16
MESH = pl.DeviceIdType.MESH


def place():
    wide = lax.axis_index("wide")
    member = lax.axis_index("narrow")
    count = lax.axis_size("wide")
    core = lax.rem(wide, 2)
    twin = wide + 1 - 2 * core
    ahead = lax.rem(wide + 2, count)
    behind = lax.rem(wide + count - 2, count)
    return wide, member, core, twin, ahead, behind


def greet(devices):
    barrier = pltpu.get_barrier_semaphore()
    for device in devices:
        pl.semaphore_signal(barrier, inc=1, device_id=device, device_id_type=MESH)
    return lambda: pl.semaphore_wait(barrier, len(devices))


def remote(src, dst, send, recv, device):
    return pltpu.make_async_remote_copy(
        src_ref=src, dst_ref=dst, send_sem=send, recv_sem=recv, device_id=device, device_id_type=MESH
    )


def list_pairs(rows, member, core):
    lane = lax.broadcasted_iota(jnp.int32, (8, FIL), 1)
    row = lax.broadcasted_iota(jnp.int32, (8, FIL), 0)
    which = lax.broadcasted_iota(jnp.int32, (8, 1), 0)
    home = which < MEMBERS
    upper = (
        lax.broadcasted_iota(jnp.int32, (FIL, FIL), 0) <= lax.broadcasted_iota(jnp.int32, (FIL, FIL), 1)
    ).astype(bf16)

    def by_row(chosen):
        return jnp.sum(chosen.astype(jnp.int32), axis=1, keepdims=True)

    def by_slab(chosen):
        counts = by_row(chosen)
        own = jnp.sum(jnp.where(home, counts, 0), axis=0, keepdims=True)
        twin = jnp.sum(jnp.where(home, 0, counts), axis=0, keepdims=True)
        return own, twin

    def rank(chosen, apart):
        inclusive = jnp.dot(chosen.astype(f32).astype(bf16), upper, preferred_element_type=f32)
        counts = by_row(chosen)
        base = jnp.zeros((8, 1), jnp.int32)
        for m in range(7):
            later = which > m
            if apart:
                later = later & (home == (m < MEMBERS))
            base = base + jnp.where(later, counts[m : m + 1], 0)
        return base + inclusive.astype(jnp.int32) - 1

    valid = rows >= 0
    offset = rows // SLAB
    quarter = (rows & (SLAB - 1)) // BLK
    source = (row & (MEMBERS - 1)) * BLK + lane // MAXP
    free = valid & (offset == 0)
    fixed = valid & (offset > 0)
    shares = [by_slab(fixed & (quarter == q)) for q in range(MEMBERS)]
    free_total = by_slab(free)
    begin, width = [], []
    for slab in range(2):
        known = [share[slab] for share in shares]
        level = (known[0] + known[1] + known[2] + known[3] + free_total[slab] + MEMBERS - 1) // MEMBERS
        room = [jnp.maximum(level - share, 0) for share in known]
        first = jnp.zeros((1, 1), jnp.int32)
        span = jnp.zeros((1, 1), jnp.int32)
        for q in range(MEMBERS):
            first = first + jnp.where(member > q, room[q], 0)
            span = span + jnp.where(member == q, room[q], 0)
        begin.append(first)
        width.append(span)
    begins = jnp.where(home, begin[0], begin[1])
    ends = begins + jnp.where(home, width[0], width[1])
    free_rank = rank(free, True)
    dealt = (fixed & (quarter == member)) | (free & (free_rank >= begins) & (free_rank < ends))
    loads = by_slab(dealt)
    movable = dealt & (quarter == member) & (source // BLK == member)
    movable_rank = rank(movable, True)
    give = jnp.maximum(loads[0] - loads[1], 0) // 2
    take = jnp.maximum(loads[1] - loads[0], 0) // 2
    crosses = movable & (movable_rank < jnp.where(home, give, take))
    mine = (dealt & home & ~crosses) | (crosses & ~home)
    spot = rank(mine, False)
    total = jnp.sum(by_row(mine), axis=0, keepdims=True)
    there = jnp.where(home, core, 1 - core)
    in_window = SLAB + (there + offset) * BLK + (rows & (BLK - 1))
    partner = jnp.where(home & (offset == 0), rows & (SLAB - 1), in_window)
    source = jnp.where(home, source, SLAB + there * BLK + (source & (BLK - 1)))
    high = jnp.where(mine, spot // 32, -1)
    low = jnp.where(mine, spot & 31, -1)
    out_i = jnp.zeros((LIST, 32), f32)
    out_j = jnp.zeros((LIST, 32), f32)
    spots_high = lax.broadcasted_iota(jnp.int32, (LIST, FIL), 0)
    spots_low = lax.broadcasted_iota(jnp.int32, (32, FIL), 0)
    contract = (((1,), (1,)), ((), ()))
    for m in range(8):
        pick_high = spots_high == high[m : m + 1]
        pick_low = (spots_low == low[m : m + 1]).astype(f32).astype(bf16)
        put_i = jnp.where(pick_high, source[m : m + 1].astype(f32), 0.0).astype(bf16)
        put_j = jnp.where(pick_high, partner[m : m + 1].astype(f32), 0.0).astype(bf16)
        out_i = out_i + lax.dot_general(put_i, pick_low, contract, preferred_element_type=f32)
        out_j = out_j + lax.dot_general(put_j, pick_low, contract, preferred_element_type=f32)
    flat = 32 * lax.broadcasted_iota(jnp.int32, (LIST, 32), 0) + lax.broadcasted_iota(jnp.int32, (LIST, 32), 1)
    used = flat < total
    li = jnp.where(used, out_i.astype(jnp.int32), ALL)
    lj = jnp.where(used, out_j.astype(jnp.int32), ALL)
    return li, lj, total


def directed(block):
    cur = block[8:ROWS]
    parts = jnp.concatenate([block[3 + comp : 4 + comp] * cur for comp in range(3)], axis=0)
    head = parts.astype(bf16)
    tail = (parts - head.astype(f32)).astype(bf16)
    return jnp.concatenate([head, tail], axis=0)


def columns(block, spread):
    geometry = jnp.concatenate([block[0:3], block[6:7] * block[6:7]], axis=0)
    head = geometry.astype(bf16).astype(f32)
    rest = geometry - head
    middle = rest.astype(bf16).astype(f32)
    tail = rest - middle
    terms = jnp.concatenate([head, middle, tail, jnp.zeros((4, FIL), f32)], axis=0)
    return jnp.dot(terms.T.astype(bf16), spread, preferred_element_type=f32)


def tile_pieces(cols, i, geometry, buf):
    radius = geometry[6:7] * geometry[6:7]

    def piece(h, r):
        cut = slice(h * 128, h * 128 + 128)
        xb, yb, zb = [jnp.broadcast_to(geometry[q : q + 1, cut], (16, 128)) for q in range(3)]
        rb = jnp.broadcast_to(radius[:, cut], (16, 128))
        xa, ya, za, ra = [cols[i, q, r : r + 16, :] for q in range(4)]
        dx, dy, dz = xa - xb, ya - yb, za - zb
        gap = (ra + rb) + dx * dx + dy * dy + dz * dz
        buf[r : r + 16, cut] = lax.rsqrt(gap).astype(bf16)

    return [functools.partial(piece, h, r) for h in range(2) for r in range(0, FIL, 16)]


def fold(product, dirs):
    both = product[0 : 3 * PORTS] + product[3 * PORTS : 6 * PORTS]
    return (
        both[0:PORTS] * dirs[0:1] + both[PORTS : 2 * PORTS] * dirs[1:2]
    ) + both[2 * PORTS : 3 * PORTS] * dirs[2:3]


def fetch_kernel(
    pos_in, dirs_in, rad_in, cur_in, target_in, count_in,
    blocks, terms, cols, acc, table,
    pos, dirs, rad, cur, target, count, in_sem, lists, tile, t_send, t_recv, y_send, y_recv, l_send, l_recv, z_send, z_recv, c_send, c_recv,
):
    wide, member, core, twin, ahead, behind = place()
    mates = [lax.rem(member + step, MEMBERS) for step in range(1, MEMBERS)]
    loads = [
        pltpu.make_async_copy(whole, held, in_sem.at[at])
        for at, (whole, held) in enumerate(
            [(pos_in, pos), (dirs_in, dirs), (rad_in, rad), (cur_in, cur), (target_in, target), (count_in, count)]
        )
    ]
    for copy in loads:
        copy.start()
    lists[...] = jnp.full((8, FIL), -1, jnp.int32)
    wait_for_greetings = greet([(wide, mate) for mate in mates] + [(ahead, member), (twin, member)])
    for copy in loads:
        copy.wait()
    slot = lax.broadcasted_iota(jnp.int32, (1, MAXP), 1)
    lists[pl.ds(member, 1)] = jnp.concatenate(
        [jnp.where(slot < count[r], target[r : r + 1], -1) for r in range(BLK)], axis=1
    )
    for b in range(BLK):
        cut = slice(b * FIL, (b + 1) * FIL)
        block = jnp.concatenate([pos[:, cut], dirs[:, cut], rad[:, cut], rad[:, cut], cur[:, cut]], axis=0)
        blocks[member * BLK + b] = block
        blocks[SLAB + core * BLK + b] = block
    wait_for_greetings()
    half = BLK // PARTS
    own = blocks.at[pl.ds(member * BLK, BLK)]

    def seat(hop, part):
        return pl.ds(SLAB + (2 * hop + core) * BLK + part * half, half)

    hops = [[]]
    for part in range(PARTS):
        copy = remote(
            blocks.at[pl.ds(member * BLK + part * half, half)], blocks.at[seat(1, part)],
            z_send.at[0, part], z_recv.at[0, part], (behind, member),
        )
        copy.start()
        hops[0].append(copy)
    list_copies = []
    for step, mate in enumerate(mates):
        row = lists.at[pl.ds(member, 1)]
        copy = remote(row, row, l_send.at[step], l_recv.at[step], (wide, mate))
        copy.start()
        list_copies.append(copy)
    unit_copies = []
    for step, mate in enumerate(mates):
        copy = remote(own, own, y_send.at[step], y_recv.at[step], (wide, mate))
        copy.start()
        unit_copies.append(copy)
    core_copies = {}
    copy = remote(own, blocks.at[pl.ds(SLAB + core * BLK, BLK)], c_send.at[0, 0], c_recv.at[0, 0], (twin, member))
    copy.start()
    core_copies[0, 0] = copy

    term = lax.broadcasted_iota(jnp.int32, (16, 512), 0)
    group = lax.broadcasted_iota(jnp.int32, (16, 512), 1) // 128
    spread = jnp.where((term < 12) & (lax.rem(term, 4) == group), 1.0, 0.0).astype(bf16)

    def ready_sources(first, held):
        @pl.loop(0, BLK // 4)
        def _(quad):
            for b in range(4):
                i = first + 4 * quad + b
                block = blocks[i]
                terms[i] = directed(block)
                wide_columns = columns(block, spread)
                for q in range(4):
                    cols[held + 4 * quad + b, q] = wide_columns[:, q * 128 : (q + 1) * 128]

    def ready_partners(first, count_of):
        @pl.loop(0, count_of // 2)
        def _(duo):
            for b in range(2):
                j = SLAB + first + 2 * duo + b
                terms[j] = directed(blocks[j])

    def pass_on(hop):
        later = []
        for part in range(PARTS):
            hops[hop - 1][part].wait_recv()
            if hop < HOPS - 1:
                copy = remote(
                    blocks.at[seat(hop, part)], blocks.at[seat(hop + 1, part)],
                    z_send.at[hop, part], z_recv.at[hop, part], (behind, member),
                )
                copy.start()
                later.append(copy)
            copy = remote(
                blocks.at[seat(hop, part)], blocks.at[seat(hop, part)],
                c_send.at[hop, part], c_recv.at[hop, part], (twin, member),
            )
            copy.start()
            core_copies[hop, part] = copy
        hops.append(later)

    def from_core(hop):
        for part in range(PARTS if hop else 1):
            core_copies[hop, part].wait_recv()

    def mate_of(step):
        return lax.rem(member + MEMBERS - 1 - step, MEMBERS)

    @pl.loop(0, ALL + 1)
    def _(i):
        acc[i] = jnp.zeros((PORTS, FIL), f32)

    ready_sources(member * BLK, member * BLK)
    for copy in list_copies:
        copy.wait()
    twin_lists = remote(
        lists.at[pl.ds(0, MEMBERS)], lists.at[pl.ds(MEMBERS, MEMBERS)], t_send, t_recv, (twin, member)
    )
    twin_lists.start()
    pass_on(1)
    twin_lists.wait()
    li, lj, total = list_pairs(lists[...], member, core)
    table[0:LIST] = li
    table[LIST : 2 * LIST] = lj
    table[2 * LIST : 2 * LIST + 8] = jnp.broadcast_to(total, (8, 32))
    for step in (0, 2):
        unit_copies[step].wait_recv()
        ready_sources(mate_of(step) * BLK, mate_of(step) * BLK)
    pass_on(2)
    unit_copies[1].wait_recv()
    ready_sources(mate_of(1) * BLK, mate_of(1) * BLK)

    @pl.loop(0, BLK)
    def _(b):
        i = member * BLK + b
        for piece in tile_pieces(cols, i, blocks[i, 0:8, :], tile):
            piece()
        product = lax.dot_general(terms[i], tile[...], (((1,), (1,)), ((), ())), preferred_element_type=f32)
        acc[i] = fold(product, blocks[i, 3:6, :])

    from_core(0)
    ready_sources(SLAB + (1 - core) * BLK, SLAB)
    ready_partners(core * BLK, BLK)
    from_core(1)
    ready_partners(2 * BLK, 2 * BLK)
    pass_on(3)
    from_core(2)
    ready_partners(4 * BLK, 2 * BLK)
    ready_partners((6 + core) * BLK, BLK)
    from_core(3)
    ready_partners((7 - core) * BLK, BLK)
    for group_of in hops:
        for copy in group_of:
            copy.wait_send()
    for copy in unit_copies + list(core_copies.values()):
        copy.wait_send()


def fetch(*inputs):
    hbm = pl.BlockSpec(memory_space=pltpu.HBM)
    vm = pl.BlockSpec(memory_space=pltpu.VMEM)
    dma = pltpu.SemaphoreType.DMA
    return pl.pallas_call(
        fetch_kernel,
        out_shape=[
            jax.ShapeDtypeStruct((ALL, ROWS, FIL), f32),
            jax.ShapeDtypeStruct((ALL, 6 * PORTS, FIL), bf16),
            jax.ShapeDtypeStruct((SLAB + BLK, 4, FIL, 128), f32),
            jax.ShapeDtypeStruct((ALL + 1, PORTS, FIL), f32),
            jax.ShapeDtypeStruct((88, 32), jnp.int32),
        ],
        in_specs=[hbm] * 6,
        out_specs=[vm] * 5,
        scratch_shapes=[
            pltpu.VMEM((3, BLK * FIL), f32),
            pltpu.VMEM((3, BLK * FIL), f32),
            pltpu.VMEM((1, BLK * FIL), f32),
            pltpu.VMEM((PORTS, BLK * FIL), f32),
            pltpu.VMEM((BLK, MAXP), jnp.int32),
            pltpu.SMEM((BLK,), jnp.int32),
            dma((6,)),
            pltpu.VMEM((8, FIL), jnp.int32),
            pltpu.VMEM((FIL, FIL), bf16),
            dma, dma,
            dma((3,)), dma((3,)), dma((3,)), dma((3,)),
            dma((3, PARTS)), dma((3, PARTS)),
            dma((HOPS, PARTS)), dma((HOPS, PARTS)),
        ],
        compiler_params=pltpu.CompilerParams(
            collective_id=0, has_side_effects=True, vmem_limit_bytes=8 * 2**20
        ),
    )(*inputs)


def tiles_kernel(table, blocks, terms, cols, start, acc, even, odd, turns, sem):
    load = pltpu.make_async_copy(table, turns, sem)
    load.start()
    load.wait()
    n = turns[2 * LIST, 0]

    def pair(k):
        row, col = k // 32, k & 31
        return turns[row, col], turns[LIST + row, col]

    def chunks(k, buf):
        i, j = pair(k)
        held = jnp.where(i < SLAB, i, SLAB + (i & (BLK - 1)))
        return tile_pieces(cols, held, blocks[jnp.minimum(j, ALL - 1), 0:8, :], buf)

    def step(k_next, buf_next, k, buf):
        work = chunks(k_next, buf_next)
        i_put, j_put = pair(k)
        i, j = jnp.minimum(i_put, ALL - 1), jnp.minimum(j_put, ALL - 1)
        behind = lax.dot_general(terms[i], buf[...], (((1,), (0,)), ((), ())), preferred_element_type=f32)
        for piece in work[:16]:
            piece()
        acc[j_put] += fold(behind, blocks[j, 3:6, :])
        ahead = lax.dot_general(terms[j], buf[...], (((1,), (1,)), ((), ())), preferred_element_type=f32)
        for piece in work[16:]:
            piece()
        acc[i_put] += fold(ahead, blocks[i, 3:6, :])

    for piece in chunks(0, even):
        piece()

    @pl.loop(0, (n + UNROLL - 1) // UNROLL)
    def _(turn):
        k = UNROLL * turn
        for q in range(UNROLL):
            now, later = (even, odd) if q % 2 == 0 else (odd, even)
            step(k + q + 1, later, k + q, now)


def tiles(table, blocks, terms, cols, acc):
    vm = pl.BlockSpec(memory_space=pltpu.VMEM)
    return pl.pallas_call(
        tiles_kernel,
        out_shape=jax.ShapeDtypeStruct((ALL + 1, PORTS, FIL), f32),
        in_specs=[vm] * 5,
        out_specs=vm,
        scratch_shapes=[
            pltpu.VMEM((FIL, FIL), bf16),
            pltpu.VMEM((FIL, FIL), bf16),
            pltpu.SMEM((88, 32), jnp.int32),
            pltpu.SemaphoreType.DMA,
        ],
        input_output_aliases={4: 0},
        compiler_params=pltpu.CompilerParams(vmem_limit_bytes=TILES_VMEM),
    )(table, blocks, terms, cols, acc)


def return_kernel(
    acc, out, x_buf, y_buf, z_buf, z_out, y_send, y_recv, z_send, z_recv, c_send, c_recv
):
    wide, member, core, twin, ahead, behind = place()
    mates = [lax.rem(member + step, MEMBERS) for step in range(1, MEMBERS)]
    first, last = wide < 2, wide >= lax.axis_size("wide") - 2
    barrier = pltpu.get_barrier_semaphore()
    for device in [(wide, mate) for mate in mates] + [(twin, member)]:
        pl.semaphore_signal(barrier, inc=1, device_id=device, device_id_type=MESH)

    @pl.when(~first)
    def _():
        pl.semaphore_signal(barrier, inc=1, device_id=(behind, member), device_id_type=MESH)

    pl.semaphore_wait(barrier, jnp.where(last, MEMBERS, MEMBERS + 1))
    half = BLK // PARTS
    core_copies = {}
    for hop in range(HOPS - 1, -1, -1):
        for part in range(PARTS):
            copy = remote(
                acc.at[pl.ds(SLAB + (2 * hop + 1 - core) * BLK + part * half, half)],
                x_buf.at[hop, pl.ds(part * half, half)],
                c_send.at[hop, part], c_recv.at[hop, part], (twin, member),
            )
            copy.start()
            core_copies[hop, part] = copy
    unit_copies = []
    for step, mate in enumerate(mates):
        copy = remote(
            acc.at[pl.ds(mate * BLK, BLK)], y_buf.at[step], y_send.at[step], y_recv.at[step], (wide, mate)
        )
        copy.start()
        unit_copies.append(copy)
    hops = {}
    for hop in range(HOPS - 1, -1, -1):
        for part in range(PARTS):
            cut = pl.ds(part * half, half)
            core_copies[hop, part].wait_recv()
            value = x_buf[hop, cut] + acc[pl.ds(SLAB + (2 * hop + core) * BLK + part * half, half)]
            if hop < HOPS - 1:
                @pl.when(~first)
                def _():
                    hops[hop + 1, part].wait_recv()

                value = value + jnp.where(first, 0.0, z_buf[hop, cut])
            if hop > 0:
                z_out[hop - 1, cut] = value
                copy = remote(
                    z_out.at[hop - 1, cut], z_buf.at[hop - 1, cut],
                    z_send.at[hop - 1, part], z_recv.at[hop - 1, part], (ahead, member),
                )
                hops[hop, part] = copy

                @pl.when(~last)
                def _():
                    copy.start()
            else:
                if part == 0:
                    for copy in unit_copies:
                        copy.wait_recv()
                value = value + acc[pl.ds(member * BLK + part * half, half)]
                for step in range(MEMBERS - 1):
                    value = value + y_buf[step, cut]
                for b in range(half):
                    at = (part * half + b) * FIL
                    out[:, at : at + FIL] = value[b]
    for copy in list(core_copies.values()) + unit_copies:
        copy.wait_send()

    @pl.when(~last)
    def _():
        for copy in hops.values():
            copy.wait_send()


def send_home(acc):
    vm = pl.BlockSpec(memory_space=pltpu.VMEM)
    dma = pltpu.SemaphoreType.DMA
    return pl.pallas_call(
        return_kernel,
        out_shape=jax.ShapeDtypeStruct((PORTS, BLK * FIL), f32),
        in_specs=[vm],
        out_specs=vm,
        scratch_shapes=[
            pltpu.VMEM((HOPS, BLK, PORTS, FIL), f32),
            pltpu.VMEM((MEMBERS - 1, BLK, PORTS, FIL), f32),
            pltpu.VMEM((HOPS - 1, BLK, PORTS, FIL), f32),
            pltpu.VMEM((HOPS - 1, BLK, PORTS, FIL), f32),
            dma((3,)), dma((3,)),
            dma((HOPS - 1, PARTS)), dma((HOPS - 1, PARTS)),
            dma((HOPS, PARTS)), dma((HOPS, PARTS)),
        ],
        compiler_params=pltpu.CompilerParams(
            collective_id=1, has_side_effects=True, vmem_limit_bytes=8 * 2**20
        ),
    )(acc)


def on_device(positions, directions, radius, currents, pair_target, pair_count):
    rad = radius.reshape(1, BLK * FIL)
    inputs = (positions, directions, rad, currents, pair_target, pair_count)
    inputs = [pltpu.with_memory_space_constraint(x, pltpu.HBM) for x in inputs]
    blocks, terms, cols, acc, table = fetch(*inputs)
    return send_home(tiles(table, blocks, terms, cols, acc))


def solution(mesh):
    return jax.shard_map(
        on_device,
        mesh=mesh,
        in_specs=(
            P(None, ("wide", "narrow")),
            P(None, ("wide", "narrow")),
            P(("wide", "narrow")),
            P(None, ("wide", "narrow")),
            P(("wide", "narrow"), None),
            P(("wide", "narrow")),
        ),
        out_specs=P(None, ("wide", "narrow")),
        check_vma=False,
    )
```

```python
import functools

import jax
import jax.numpy as jnp
from jax import lax
from jax.experimental import pallas as pl
from jax.experimental.pallas import tpu as pltpu
from jax.sharding import PartitionSpec as P

FIL = 256
PORTS = 16
BLK = 8
MAXP = 32
SLAB = 32
MEMBERS = 4
HOPS = 4
ROWS = 24
WINDOW = 2 * HOPS * BLK
ALL = SLAB + WINDOW
LIST = 40
UNROLL = 8
PARTS = 4
TILES_VMEM = 4 * 2**20
f32 = jnp.float32
bf16 = jnp.bfloat16
MESH = pl.DeviceIdType.MESH


def place():
    wide = lax.axis_index("wide")
    member = lax.axis_index("narrow")
    count = lax.axis_size("wide")
    core = lax.rem(wide, 2)
    twin = wide + 1 - 2 * core
    ahead = lax.rem(wide + 2, count)
    behind = lax.rem(wide + count - 2, count)
    return wide, member, core, twin, ahead, behind


def greet(devices):
    barrier = pltpu.get_barrier_semaphore()
    for device in devices:
        pl.semaphore_signal(barrier, inc=1, device_id=device, device_id_type=MESH)
    return lambda: pl.semaphore_wait(barrier, len(devices))


def remote(src, dst, send, recv, device):
    return pltpu.make_async_remote_copy(
        src_ref=src, dst_ref=dst, send_sem=send, recv_sem=recv, device_id=device, device_id_type=MESH
    )


def list_pairs(rows, member, core):
    lane = lax.broadcasted_iota(jnp.int32, (8, FIL), 1)
    row = lax.broadcasted_iota(jnp.int32, (8, FIL), 0)
    which = lax.broadcasted_iota(jnp.int32, (8, 1), 0)
    home = which < MEMBERS
    upper = (
        lax.broadcasted_iota(jnp.int32, (FIL, FIL), 0) <= lax.broadcasted_iota(jnp.int32, (FIL, FIL), 1)
    ).astype(bf16)

    def by_row(chosen):
        return jnp.sum(chosen.astype(jnp.int32), axis=1, keepdims=True)

    def by_slab(chosen):
        counts = by_row(chosen)
        own = jnp.sum(jnp.where(home, counts, 0), axis=0, keepdims=True)
        twin = jnp.sum(jnp.where(home, 0, counts), axis=0, keepdims=True)
        return own, twin

    def rank(chosen, apart):
        inclusive = jnp.dot(chosen.astype(f32).astype(bf16), upper, preferred_element_type=f32)
        counts = by_row(chosen)
        base = jnp.zeros((8, 1), jnp.int32)
        for m in range(7):
            later = which > m
            if apart:
                later = later & (home == (m < MEMBERS))
            base = base + jnp.where(later, counts[m : m + 1], 0)
        return base + inclusive.astype(jnp.int32) - 1

    valid = rows >= 0
    offset = rows // SLAB
    quarter = (rows & (SLAB - 1)) // BLK
    source = (row & (MEMBERS - 1)) * BLK + lane // MAXP
    free = valid & (offset == 0)
    fixed = valid & (offset > 0)
    shares = [by_slab(fixed & (quarter == q)) for q in range(MEMBERS)]
    free_total = by_slab(free)
    begin, width = [], []
    for slab in range(2):
        known = [share[slab] for share in shares]
        level = (known[0] + known[1] + known[2] + known[3] + free_total[slab] + MEMBERS - 1) // MEMBERS
        room = [jnp.maximum(level - share, 0) for share in known]
        first = jnp.zeros((1, 1), jnp.int32)
        span = jnp.zeros((1, 1), jnp.int32)
        for q in range(MEMBERS):
            first = first + jnp.where(member > q, room[q], 0)
            span = span + jnp.where(member == q, room[q], 0)
        begin.append(first)
        width.append(span)
    begins = jnp.where(home, begin[0], begin[1])
    ends = begins + jnp.where(home, width[0], width[1])
    free_rank = rank(free, True)
    dealt = (fixed & (quarter == member)) | (free & (free_rank >= begins) & (free_rank < ends))
    loads = by_slab(dealt)
    movable = dealt & (quarter == member) & (source // BLK == member)
    movable_rank = rank(movable, True)
    give = jnp.maximum(loads[0] - loads[1], 0) // 2
    take = jnp.maximum(loads[1] - loads[0], 0) // 2
    crosses = movable & (movable_rank < jnp.where(home, give, take))
    mine = (dealt & home & ~crosses) | (crosses & ~home)
    spot = rank(mine, False)
    total = jnp.sum(by_row(mine), axis=0, keepdims=True)
    there = jnp.where(home, core, 1 - core)
    in_window = SLAB + (there + offset) * BLK + (rows & (BLK - 1))
    partner = jnp.where(home & (offset == 0), rows & (SLAB - 1), in_window)
    source = jnp.where(home, source, SLAB + there * BLK + (source & (BLK - 1)))
    high = jnp.where(mine, spot // 32, -1)
    low = jnp.where(mine, spot & 31, -1)
    out_i = jnp.zeros((LIST, 32), f32)
    out_j = jnp.zeros((LIST, 32), f32)
    spots_high = lax.broadcasted_iota(jnp.int32, (LIST, FIL), 0)
    spots_low = lax.broadcasted_iota(jnp.int32, (32, FIL), 0)
    contract = (((1,), (1,)), ((), ()))
    for m in range(8):
        pick_high = spots_high == high[m : m + 1]
        pick_low = (spots_low == low[m : m + 1]).astype(f32).astype(bf16)
        put_i = jnp.where(pick_high, source[m : m + 1].astype(f32), 0.0).astype(bf16)
        put_j = jnp.where(pick_high, partner[m : m + 1].astype(f32), 0.0).astype(bf16)
        out_i = out_i + lax.dot_general(put_i, pick_low, contract, preferred_element_type=f32)
        out_j = out_j + lax.dot_general(put_j, pick_low, contract, preferred_element_type=f32)
    flat = 32 * lax.broadcasted_iota(jnp.int32, (LIST, 32), 0) + lax.broadcasted_iota(jnp.int32, (LIST, 32), 1)
    used = flat < total
    li = jnp.where(used, out_i.astype(jnp.int32), ALL)
    lj = jnp.where(used, out_j.astype(jnp.int32), ALL)
    return li, lj, total


def directed(block):
    cur = block[8:ROWS]
    parts = jnp.concatenate([block[3 + comp : 4 + comp] * cur for comp in range(3)], axis=0)
    head = parts.astype(bf16)
    tail = (parts - head.astype(f32)).astype(bf16)
    return jnp.concatenate([head, tail], axis=0)


def depth_base(wide):
    return (wide // 2).astype(f32) * 0.2 + 0.5


def columns(block, spread, base):
    depth = block[2:3] - base
    geometry = jnp.concatenate([block[0:2], -2.0 * depth, block[6:7] * block[6:7] + depth * depth], axis=0)
    head = geometry.astype(bf16).astype(f32)
    rest = geometry - head
    middle = rest.astype(bf16).astype(f32)
    tail = rest - middle
    terms = jnp.concatenate([head, middle, tail, jnp.zeros((4, FIL), f32)], axis=0)
    return jnp.dot(terms.T.astype(bf16), spread, preferred_element_type=f32)


def tile_pieces(cols, i, geometry, base, buf):
    depth = geometry[2:3] - base
    sized = geometry[6:7] * geometry[6:7] + depth * depth

    def piece(h, r):
        cut = slice(h * 128, h * 128 + 128)
        xb, yb, zb, rb = [jnp.broadcast_to(v[:, cut], (16, 128)) for v in (geometry[0:1], geometry[1:2], depth, sized)]
        xa, ya, za, ra = [cols[i, q, r : r + 16, :] for q in range(4)]
        dx, dy = xa - xb, ya - yb
        gap = ((ra + rb) + za * zb) + dx * dx + dy * dy
        buf[r : r + 16, cut] = lax.rsqrt(gap).astype(bf16)

    return [functools.partial(piece, h, r) for h in range(2) for r in range(0, FIL, 16)]


def fold(product, dirs):
    both = product[0 : 3 * PORTS] + product[3 * PORTS : 6 * PORTS]
    return (
        both[0:PORTS] * dirs[0:1] + both[PORTS : 2 * PORTS] * dirs[1:2]
    ) + both[2 * PORTS : 3 * PORTS] * dirs[2:3]


def fetch_kernel(
    pos_in, dirs_in, rad_in, cur_in, target_in, count_in,
    blocks, terms, cols, acc, table,
    pos, dirs, rad, cur, target, count, in_sem, lists, tile, t_send, t_recv, y_send, y_recv, l_send, l_recv, z_send, z_recv, c_send, c_recv,
):
    wide, member, core, twin, ahead, behind = place()
    mates = [lax.rem(member + step, MEMBERS) for step in range(1, MEMBERS)]
    loads = [
        pltpu.make_async_copy(whole, held, in_sem.at[at])
        for at, (whole, held) in enumerate(
            [(pos_in, pos), (dirs_in, dirs), (rad_in, rad), (cur_in, cur), (target_in, target), (count_in, count)]
        )
    ]
    for copy in loads:
        copy.start()
    lists[...] = jnp.full((8, FIL), -1, jnp.int32)
    wait_for_greetings = greet([(wide, mate) for mate in mates] + [(ahead, member), (twin, member)])
    for copy in loads:
        copy.wait()
    slot = lax.broadcasted_iota(jnp.int32, (1, MAXP), 1)
    lists[pl.ds(member, 1)] = jnp.concatenate(
        [jnp.where(slot < count[r], target[r : r + 1], -1) for r in range(BLK)], axis=1
    )
    for b in range(BLK):
        cut = slice(b * FIL, (b + 1) * FIL)
        block = jnp.concatenate([pos[:, cut], dirs[:, cut], rad[:, cut], rad[:, cut], cur[:, cut]], axis=0)
        blocks[member * BLK + b] = block
        blocks[SLAB + core * BLK + b] = block
    wait_for_greetings()
    half = BLK // PARTS
    own = blocks.at[pl.ds(member * BLK, BLK)]

    def seat(hop, part):
        return pl.ds(SLAB + (2 * hop + core) * BLK + part * half, half)

    hops = [[]]
    for part in range(PARTS):
        copy = remote(
            blocks.at[pl.ds(member * BLK + part * half, half)], blocks.at[seat(1, part)],
            z_send.at[0, part], z_recv.at[0, part], (behind, member),
        )
        copy.start()
        hops[0].append(copy)
    list_copies = []
    for step, mate in enumerate(mates):
        row = lists.at[pl.ds(member, 1)]
        copy = remote(row, row, l_send.at[step], l_recv.at[step], (wide, mate))
        copy.start()
        list_copies.append(copy)
    unit_copies = []
    for step, mate in enumerate(mates):
        copy = remote(own, own, y_send.at[step], y_recv.at[step], (wide, mate))
        copy.start()
        unit_copies.append(copy)
    core_copies = {}
    copy = remote(own, blocks.at[pl.ds(SLAB + core * BLK, BLK)], c_send.at[0, 0], c_recv.at[0, 0], (twin, member))
    copy.start()
    core_copies[0, 0] = copy

    base = depth_base(wide)
    term = lax.broadcasted_iota(jnp.int32, (16, 512), 0)
    group = lax.broadcasted_iota(jnp.int32, (16, 512), 1) // 128
    spread = jnp.where((term < 12) & (lax.rem(term, 4) == group), 1.0, 0.0).astype(bf16)

    def ready_sources(first, held):
        @pl.loop(0, BLK // 4)
        def _(quad):
            for b in range(4):
                i = first + 4 * quad + b
                block = blocks[i]
                terms[i] = directed(block)
                wide_columns = columns(block, spread, base)
                for q in range(4):
                    cols[held + 4 * quad + b, q] = wide_columns[:, q * 128 : (q + 1) * 128]

    def ready_partners(first, count_of):
        @pl.loop(0, count_of // 2)
        def _(duo):
            for b in range(2):
                j = SLAB + first + 2 * duo + b
                terms[j] = directed(blocks[j])

    def pass_on(hop):
        later = []
        for part in range(PARTS):
            hops[hop - 1][part].wait_recv()
            if hop < HOPS - 1:
                copy = remote(
                    blocks.at[seat(hop, part)], blocks.at[seat(hop + 1, part)],
                    z_send.at[hop, part], z_recv.at[hop, part], (behind, member),
                )
                copy.start()
                later.append(copy)
            copy = remote(
                blocks.at[seat(hop, part)], blocks.at[seat(hop, part)],
                c_send.at[hop, part], c_recv.at[hop, part], (twin, member),
            )
            copy.start()
            core_copies[hop, part] = copy
        hops.append(later)

    def from_core(hop):
        for part in range(PARTS if hop else 1):
            core_copies[hop, part].wait_recv()

    def mate_of(step):
        return lax.rem(member + MEMBERS - 1 - step, MEMBERS)

    @pl.loop(0, ALL + 1)
    def _(i):
        acc[i] = jnp.zeros((PORTS, FIL), f32)

    ready_sources(member * BLK, member * BLK)
    for copy in list_copies:
        copy.wait()
    twin_lists = remote(
        lists.at[pl.ds(0, MEMBERS)], lists.at[pl.ds(MEMBERS, MEMBERS)], t_send, t_recv, (twin, member)
    )
    twin_lists.start()
    pass_on(1)
    twin_lists.wait()
    li, lj, total = list_pairs(lists[...], member, core)
    table[0:LIST] = li
    table[LIST : 2 * LIST] = lj
    table[2 * LIST : 2 * LIST + 8] = jnp.broadcast_to(total, (8, 32))
    for step in (0, 2):
        unit_copies[step].wait_recv()
        ready_sources(mate_of(step) * BLK, mate_of(step) * BLK)
    pass_on(2)
    unit_copies[1].wait_recv()
    ready_sources(mate_of(1) * BLK, mate_of(1) * BLK)

    @pl.loop(0, BLK)
    def _(b):
        i = member * BLK + b
        for piece in tile_pieces(cols, i, blocks[i, 0:8, :], base, tile):
            piece()
        product = lax.dot_general(terms[i], tile[...], (((1,), (1,)), ((), ())), preferred_element_type=f32)
        acc[i] = fold(product, blocks[i, 3:6, :])

    from_core(0)
    ready_sources(SLAB + (1 - core) * BLK, SLAB)
    ready_partners(core * BLK, BLK)
    from_core(1)
    ready_partners(2 * BLK, 2 * BLK)
    pass_on(3)
    from_core(2)
    ready_partners(4 * BLK, 2 * BLK)
    ready_partners((6 + core) * BLK, BLK)
    from_core(3)
    ready_partners((7 - core) * BLK, BLK)
    for group_of in hops:
        for copy in group_of:
            copy.wait_send()
    for copy in unit_copies + list(core_copies.values()):
        copy.wait_send()


def fetch(*inputs):
    hbm = pl.BlockSpec(memory_space=pltpu.HBM)
    vm = pl.BlockSpec(memory_space=pltpu.VMEM)
    dma = pltpu.SemaphoreType.DMA
    return pl.pallas_call(
        fetch_kernel,
        out_shape=[
            jax.ShapeDtypeStruct((ALL, ROWS, FIL), f32),
            jax.ShapeDtypeStruct((ALL, 6 * PORTS, FIL), bf16),
            jax.ShapeDtypeStruct((SLAB + BLK, 4, FIL, 128), f32),
            jax.ShapeDtypeStruct((ALL + 1, PORTS, FIL), f32),
            jax.ShapeDtypeStruct((88, 32), jnp.int32),
        ],
        in_specs=[hbm] * 6,
        out_specs=[vm] * 5,
        scratch_shapes=[
            pltpu.VMEM((3, BLK * FIL), f32),
            pltpu.VMEM((3, BLK * FIL), f32),
            pltpu.VMEM((1, BLK * FIL), f32),
            pltpu.VMEM((PORTS, BLK * FIL), f32),
            pltpu.VMEM((BLK, MAXP), jnp.int32),
            pltpu.SMEM((BLK,), jnp.int32),
            dma((6,)),
            pltpu.VMEM((8, FIL), jnp.int32),
            pltpu.VMEM((FIL, FIL), bf16),
            dma, dma,
            dma((3,)), dma((3,)), dma((3,)), dma((3,)),
            dma((3, PARTS)), dma((3, PARTS)),
            dma((HOPS, PARTS)), dma((HOPS, PARTS)),
        ],
        compiler_params=pltpu.CompilerParams(
            collective_id=0, has_side_effects=True, vmem_limit_bytes=8 * 2**20
        ),
    )(*inputs)


def tiles_kernel(table, blocks, terms, cols, start, acc, even, odd, turns, sem):
    load = pltpu.make_async_copy(table, turns, sem)
    load.start()
    load.wait()
    n = turns[2 * LIST, 0]
    base = depth_base(lax.axis_index("wide"))

    def pair(k):
        row, col = k // 32, k & 31
        return turns[row, col], turns[LIST + row, col]

    def chunks(k, buf):
        i, j = pair(k)
        held = jnp.where(i < SLAB, i, SLAB + (i & (BLK - 1)))
        return tile_pieces(cols, held, blocks[jnp.minimum(j, ALL - 1), 0:8, :], base, buf)

    def step(k_next, buf_next, k, buf):
        work = chunks(k_next, buf_next)
        i_put, j_put = pair(k)
        i, j = jnp.minimum(i_put, ALL - 1), jnp.minimum(j_put, ALL - 1)
        behind = lax.dot_general(terms[i], buf[...], (((1,), (0,)), ((), ())), preferred_element_type=f32)
        for piece in work[:16]:
            piece()
        acc[j_put] += fold(behind, blocks[j, 3:6, :])
        ahead = lax.dot_general(terms[j], buf[...], (((1,), (1,)), ((), ())), preferred_element_type=f32)
        for piece in work[16:]:
            piece()
        acc[i_put] += fold(ahead, blocks[i, 3:6, :])

    for piece in chunks(0, even):
        piece()

    def steps(k, count):
        for q in range(count):
            now, later = (even, odd) if q % 2 == 0 else (odd, even)
            step(k + q + 1, later, k + q, now)

    half = UNROLL // 2

    @pl.loop(0, (n + half - 1) // UNROLL)
    def _(turn):
        steps(UNROLL * turn, UNROLL)

    left = n & (UNROLL - 1)

    @pl.when((left > 0) & (left <= half))
    def _():
        steps(n - left, half)


def tiles(table, blocks, terms, cols, acc):
    vm = pl.BlockSpec(memory_space=pltpu.VMEM)
    return pl.pallas_call(
        tiles_kernel,
        out_shape=jax.ShapeDtypeStruct((ALL + 1, PORTS, FIL), f32),
        in_specs=[vm] * 5,
        out_specs=vm,
        scratch_shapes=[
            pltpu.VMEM((FIL, FIL), bf16),
            pltpu.VMEM((FIL, FIL), bf16),
            pltpu.SMEM((88, 32), jnp.int32),
            pltpu.SemaphoreType.DMA,
        ],
        input_output_aliases={4: 0},
        compiler_params=pltpu.CompilerParams(vmem_limit_bytes=TILES_VMEM),
    )(table, blocks, terms, cols, acc)


def return_kernel(
    acc, out, x_buf, y_buf, z_buf, z_out, y_send, y_recv, z_send, z_recv, c_send, c_recv
):
    wide, member, core, twin, ahead, behind = place()
    mates = [lax.rem(member + step, MEMBERS) for step in range(1, MEMBERS)]
    first, last = wide < 2, wide >= lax.axis_size("wide") - 2
    barrier = pltpu.get_barrier_semaphore()
    for device in [(wide, mate) for mate in mates] + [(twin, member)]:
        pl.semaphore_signal(barrier, inc=1, device_id=device, device_id_type=MESH)

    @pl.when(~first)
    def _():
        pl.semaphore_signal(barrier, inc=1, device_id=(behind, member), device_id_type=MESH)

    pl.semaphore_wait(barrier, jnp.where(last, MEMBERS, MEMBERS + 1))
    half = BLK // PARTS
    core_copies = {}
    for hop in range(HOPS - 1, -1, -1):
        for part in range(PARTS):
            copy = remote(
                acc.at[pl.ds(SLAB + (2 * hop + 1 - core) * BLK + part * half, half)],
                x_buf.at[hop, pl.ds(part * half, half)],
                c_send.at[hop, part], c_recv.at[hop, part], (twin, member),
            )
            copy.start()
            core_copies[hop, part] = copy
    unit_copies = []
    for step, mate in enumerate(mates):
        copy = remote(
            acc.at[pl.ds(mate * BLK, BLK)], y_buf.at[step], y_send.at[step], y_recv.at[step], (wide, mate)
        )
        copy.start()
        unit_copies.append(copy)
    hops = {}
    for hop in range(HOPS - 1, -1, -1):
        for part in range(PARTS):
            cut = pl.ds(part * half, half)
            core_copies[hop, part].wait_recv()
            value = x_buf[hop, cut] + acc[pl.ds(SLAB + (2 * hop + core) * BLK + part * half, half)]
            if hop < HOPS - 1:
                @pl.when(~first)
                def _():
                    hops[hop + 1, part].wait_recv()

                value = value + jnp.where(first, 0.0, z_buf[hop, cut])
            if hop > 0:
                z_out[hop - 1, cut] = value
                copy = remote(
                    z_out.at[hop - 1, cut], z_buf.at[hop - 1, cut],
                    z_send.at[hop - 1, part], z_recv.at[hop - 1, part], (ahead, member),
                )
                hops[hop, part] = copy

                @pl.when(~last)
                def _():
                    copy.start()
            else:
                if part == 0:
                    for copy in unit_copies:
                        copy.wait_recv()
                value = value + acc[pl.ds(member * BLK + part * half, half)]
                for step in range(MEMBERS - 1):
                    value = value + y_buf[step, cut]
                for b in range(half):
                    at = (part * half + b) * FIL
                    out[:, at : at + FIL] = value[b]
    for copy in list(core_copies.values()) + unit_copies:
        copy.wait_send()

    @pl.when(~last)
    def _():
        for copy in hops.values():
            copy.wait_send()


def send_home(acc):
    vm = pl.BlockSpec(memory_space=pltpu.VMEM)
    dma = pltpu.SemaphoreType.DMA
    return pl.pallas_call(
        return_kernel,
        out_shape=jax.ShapeDtypeStruct((PORTS, BLK * FIL), f32),
        in_specs=[vm],
        out_specs=vm,
        scratch_shapes=[
            pltpu.VMEM((HOPS, BLK, PORTS, FIL), f32),
            pltpu.VMEM((MEMBERS - 1, BLK, PORTS, FIL), f32),
            pltpu.VMEM((HOPS - 1, BLK, PORTS, FIL), f32),
            pltpu.VMEM((HOPS - 1, BLK, PORTS, FIL), f32),
            dma((3,)), dma((3,)),
            dma((HOPS - 1, PARTS)), dma((HOPS - 1, PARTS)),
            dma((HOPS, PARTS)), dma((HOPS, PARTS)),
        ],
        compiler_params=pltpu.CompilerParams(
            collective_id=1, has_side_effects=True, vmem_limit_bytes=8 * 2**20
        ),
    )(acc)


def on_device(positions, directions, radius, currents, pair_target, pair_count):
    rad = radius.reshape(1, BLK * FIL)
    inputs = (positions, directions, rad, currents, pair_target, pair_count)
    inputs = [pltpu.with_memory_space_constraint(x, pltpu.HBM) for x in inputs]
    blocks, terms, cols, acc, table = fetch(*inputs)
    return send_home(tiles(table, blocks, terms, cols, acc))


def solution(mesh):
    return jax.shard_map(
        on_device,
        mesh=mesh,
        in_specs=(
            P(None, ("wide", "narrow")),
            P(None, ("wide", "narrow")),
            P(("wide", "narrow")),
            P(None, ("wide", "narrow")),
            P(("wide", "narrow"), None),
            P(("wide", "narrow")),
        ),
        out_specs=P(None, ("wide", "narrow")),
        check_vma=False,
    )
```

```python
import functools

import jax
import jax.numpy as jnp
from jax import lax
from jax.experimental import pallas as pl
from jax.experimental.pallas import tpu as pltpu
from jax.sharding import PartitionSpec as P

FIL = 256
PORTS = 16
BLK = 8
MAXP = 32
SLAB = 32
MEMBERS = 4
HOPS = 4
ROWS = 24
WINDOW = 2 * HOPS * BLK
ALL = SLAB + WINDOW
LIST = 40
UNROLL = 8
PARTS = 4
TILES_VMEM = 4 * 2**20
f32 = jnp.float32
bf16 = jnp.bfloat16
MESH = pl.DeviceIdType.MESH


def place():
    wide = lax.axis_index("wide")
    member = lax.axis_index("narrow")
    count = lax.axis_size("wide")
    core = lax.rem(wide, 2)
    twin = wide + 1 - 2 * core
    ahead = lax.rem(wide + 2, count)
    behind = lax.rem(wide + count - 2, count)
    return wide, member, core, twin, ahead, behind


def greet(devices):
    barrier = pltpu.get_barrier_semaphore()
    for device in devices:
        pl.semaphore_signal(barrier, inc=1, device_id=device, device_id_type=MESH)
    return lambda: pl.semaphore_wait(barrier, len(devices))


def remote(src, dst, send, recv, device):
    return pltpu.make_async_remote_copy(
        src_ref=src, dst_ref=dst, send_sem=send, recv_sem=recv, device_id=device, device_id_type=MESH
    )


def list_pairs(rows, member, core):
    lane = lax.broadcasted_iota(jnp.int32, (8, FIL), 1)
    row = lax.broadcasted_iota(jnp.int32, (8, FIL), 0)
    which = lax.broadcasted_iota(jnp.int32, (8, 1), 0)
    home = which < MEMBERS
    upper = (
        lax.broadcasted_iota(jnp.int32, (FIL, FIL), 0) <= lax.broadcasted_iota(jnp.int32, (FIL, FIL), 1)
    ).astype(bf16)

    def by_row(chosen):
        return jnp.sum(chosen.astype(jnp.int32), axis=1, keepdims=True)

    def by_slab(chosen):
        counts = by_row(chosen)
        own = jnp.sum(jnp.where(home, counts, 0), axis=0, keepdims=True)
        twin = jnp.sum(jnp.where(home, 0, counts), axis=0, keepdims=True)
        return own, twin

    def rank(chosen, apart):
        inclusive = jnp.dot(chosen.astype(f32).astype(bf16), upper, preferred_element_type=f32)
        counts = by_row(chosen)
        base = jnp.zeros((8, 1), jnp.int32)
        for m in range(7):
            later = which > m
            if apart:
                later = later & (home == (m < MEMBERS))
            base = base + jnp.where(later, counts[m : m + 1], 0)
        return base + inclusive.astype(jnp.int32) - 1

    valid = rows >= 0
    offset = rows // SLAB
    quarter = (rows & (SLAB - 1)) // BLK
    source = (row & (MEMBERS - 1)) * BLK + lane // MAXP
    free = valid & (offset == 0)
    fixed = valid & (offset > 0)
    shares = [by_slab(fixed & (quarter == q)) for q in range(MEMBERS)]
    free_total = by_slab(free)
    begin, width = [], []
    for slab in range(2):
        known = [share[slab] for share in shares]
        level = (known[0] + known[1] + known[2] + known[3] + free_total[slab] + MEMBERS - 1) // MEMBERS
        room = [jnp.maximum(level - share, 0) for share in known]
        first = jnp.zeros((1, 1), jnp.int32)
        span = jnp.zeros((1, 1), jnp.int32)
        for q in range(MEMBERS):
            first = first + jnp.where(member > q, room[q], 0)
            span = span + jnp.where(member == q, room[q], 0)
        begin.append(first)
        width.append(span)
    begins = jnp.where(home, begin[0], begin[1])
    ends = begins + jnp.where(home, width[0], width[1])
    free_rank = rank(free, True)
    dealt = (fixed & (quarter == member)) | (free & (free_rank >= begins) & (free_rank < ends))
    loads = by_slab(dealt)
    movable = dealt & (quarter == member) & (source // BLK == member)
    movable_rank = rank(movable, True)
    give = jnp.maximum(loads[0] - loads[1], 0) // 2
    take = jnp.maximum(loads[1] - loads[0], 0) // 2
    crosses = movable & (movable_rank < jnp.where(home, give, take))
    mine = (dealt & home & ~crosses) | (crosses & ~home)
    spot = rank(mine, False)
    total = jnp.sum(by_row(mine), axis=0, keepdims=True)
    there = jnp.where(home, core, 1 - core)
    in_window = SLAB + (there + offset) * BLK + (rows & (BLK - 1))
    partner = jnp.where(home & (offset == 0), rows & (SLAB - 1), in_window)
    source = jnp.where(home, source, SLAB + there * BLK + (source & (BLK - 1)))
    high = jnp.where(mine, spot // 32, -1)
    low = jnp.where(mine, spot & 31, -1)
    out_i = jnp.zeros((LIST, 32), f32)
    out_j = jnp.zeros((LIST, 32), f32)
    spots_high = lax.broadcasted_iota(jnp.int32, (LIST, FIL), 0)
    spots_low = lax.broadcasted_iota(jnp.int32, (32, FIL), 0)
    contract = (((1,), (1,)), ((), ()))
    for m in range(8):
        pick_high = spots_high == high[m : m + 1]
        pick_low = (spots_low == low[m : m + 1]).astype(f32).astype(bf16)
        put_i = jnp.where(pick_high, source[m : m + 1].astype(f32), 0.0).astype(bf16)
        put_j = jnp.where(pick_high, partner[m : m + 1].astype(f32), 0.0).astype(bf16)
        out_i = out_i + lax.dot_general(put_i, pick_low, contract, preferred_element_type=f32)
        out_j = out_j + lax.dot_general(put_j, pick_low, contract, preferred_element_type=f32)
    flat = 32 * lax.broadcasted_iota(jnp.int32, (LIST, 32), 0) + lax.broadcasted_iota(jnp.int32, (LIST, 32), 1)
    used = flat < total
    li = jnp.where(used, out_i.astype(jnp.int32), ALL)
    lj = jnp.where(used, out_j.astype(jnp.int32), ALL)
    return li, lj, total


def directed(block):
    cur = block[8:ROWS]
    parts = jnp.concatenate([block[3 + comp : 4 + comp] * cur for comp in range(3)], axis=0)
    head = parts.astype(bf16)
    tail = (parts - head.astype(f32)).astype(bf16)
    return jnp.concatenate([head, tail], axis=0)


def depth_base(wide):
    return (wide // 2).astype(f32) * 0.2 + 0.5


def columns(block, spread, base):
    depth = block[2:3] - base
    geometry = jnp.concatenate([block[0:2], -2.0 * depth, block[6:7] * block[6:7] + depth * depth], axis=0)
    head = geometry.astype(bf16).astype(f32)
    rest = geometry - head
    middle = rest.astype(bf16).astype(f32)
    tail = rest - middle
    terms = jnp.concatenate([head, middle, tail, jnp.zeros((4, FIL), f32)], axis=0)
    return jnp.dot(terms.T.astype(bf16), spread, preferred_element_type=f32)


def tile_pieces(cols, i, geometry, base, buf):
    depth = geometry[2:3] - base
    sized = geometry[6:7] * geometry[6:7] + depth * depth

    def piece(r):
        xa, ya, za, ra = [cols[i, q, r : r + 16, :] for q in range(4)]
        halves = []
        for h in range(2):
            cut = slice(h * 128, h * 128 + 128)
            xb, yb, zb, rb = [
                jnp.broadcast_to(v[:, cut], (16, 128)) for v in (geometry[0:1], geometry[1:2], depth, sized)
            ]
            dx, dy = xa - xb, ya - yb
            gap = ((ra + rb) + za * zb) + dx * dx + dy * dy
            halves.append(lax.rsqrt(gap).astype(bf16))
        buf[r : r + 16, :] = jnp.concatenate(halves, axis=1)

    return [functools.partial(piece, r) for r in range(0, FIL, 16)]


def fold(product, dirs):
    both = product[0 : 3 * PORTS] + product[3 * PORTS : 6 * PORTS]
    return (
        both[0:PORTS] * dirs[0:1] + both[PORTS : 2 * PORTS] * dirs[1:2]
    ) + both[2 * PORTS : 3 * PORTS] * dirs[2:3]


def fetch_kernel(
    pos_in, dirs_in, rad_in, cur_in, target_in, count_in,
    blocks, terms, cols, acc, table,
    pos, dirs, rad, cur, target, count, in_sem, lists, tile, t_send, t_recv, y_send, y_recv, l_send, l_recv, z_send, z_recv, c_send, c_recv,
):
    wide, member, core, twin, ahead, behind = place()
    mates = [lax.rem(member + step, MEMBERS) for step in range(1, MEMBERS)]
    loads = [
        pltpu.make_async_copy(whole, held, in_sem.at[at])
        for at, (whole, held) in enumerate(
            [(pos_in, pos), (dirs_in, dirs), (rad_in, rad), (cur_in, cur), (target_in, target), (count_in, count)]
        )
    ]
    for copy in loads:
        copy.start()
    lists[...] = jnp.full((8, FIL), -1, jnp.int32)
    wait_for_greetings = greet([(wide, mate) for mate in mates] + [(ahead, member), (twin, member)])
    for copy in loads:
        copy.wait()
    slot = lax.broadcasted_iota(jnp.int32, (1, MAXP), 1)
    lists[pl.ds(member, 1)] = jnp.concatenate(
        [jnp.where(slot < count[r], target[r : r + 1], -1) for r in range(BLK)], axis=1
    )
    for b in range(BLK):
        cut = slice(b * FIL, (b + 1) * FIL)
        block = jnp.concatenate([pos[:, cut], dirs[:, cut], rad[:, cut], rad[:, cut], cur[:, cut]], axis=0)
        blocks[member * BLK + b] = block
        blocks[SLAB + core * BLK + b] = block
    wait_for_greetings()
    half = BLK // PARTS
    own = blocks.at[pl.ds(member * BLK, BLK)]

    def seat(hop, part):
        return pl.ds(SLAB + (2 * hop + core) * BLK + part * half, half)

    hops = [[]]
    for part in range(PARTS):
        copy = remote(
            blocks.at[pl.ds(member * BLK + part * half, half)], blocks.at[seat(1, part)],
            z_send.at[0, part], z_recv.at[0, part], (behind, member),
        )
        copy.start()
        hops[0].append(copy)
    list_copies = []
    for step, mate in enumerate(mates):
        row = lists.at[pl.ds(member, 1)]
        copy = remote(row, row, l_send.at[step], l_recv.at[step], (wide, mate))
        copy.start()
        list_copies.append(copy)
    unit_copies = []
    for step, mate in enumerate(mates):
        copy = remote(own, own, y_send.at[step], y_recv.at[step], (wide, mate))
        copy.start()
        unit_copies.append(copy)
    core_copies = {}
    copy = remote(own, blocks.at[pl.ds(SLAB + core * BLK, BLK)], c_send.at[0, 0], c_recv.at[0, 0], (twin, member))
    copy.start()
    core_copies[0, 0] = copy

    base = depth_base(wide)
    term = lax.broadcasted_iota(jnp.int32, (16, 512), 0)
    group = lax.broadcasted_iota(jnp.int32, (16, 512), 1) // 128
    spread = jnp.where((term < 12) & (lax.rem(term, 4) == group), 1.0, 0.0).astype(bf16)

    def ready_sources(first, held):
        @pl.loop(0, BLK // 4)
        def _(quad):
            for b in range(4):
                i = first + 4 * quad + b
                block = blocks[i]
                terms[i] = directed(block)
                wide_columns = columns(block, spread, base)
                for q in range(4):
                    cols[held + 4 * quad + b, q] = wide_columns[:, q * 128 : (q + 1) * 128]

    def ready_partners(first, count_of):
        @pl.loop(0, count_of // 2)
        def _(duo):
            for b in range(2):
                j = SLAB + first + 2 * duo + b
                terms[j] = directed(blocks[j])

    def pass_on(hop):
        later = []
        for part in range(PARTS):
            hops[hop - 1][part].wait_recv()
            if hop < HOPS - 1:
                copy = remote(
                    blocks.at[seat(hop, part)], blocks.at[seat(hop + 1, part)],
                    z_send.at[hop, part], z_recv.at[hop, part], (behind, member),
                )
                copy.start()
                later.append(copy)
            copy = remote(
                blocks.at[seat(hop, part)], blocks.at[seat(hop, part)],
                c_send.at[hop, part], c_recv.at[hop, part], (twin, member),
            )
            copy.start()
            core_copies[hop, part] = copy
        hops.append(later)

    def from_core(hop):
        for part in range(PARTS if hop else 1):
            core_copies[hop, part].wait_recv()

    def mate_of(step):
        return lax.rem(member + MEMBERS - 1 - step, MEMBERS)

    @pl.loop(0, ALL + 1)
    def _(i):
        acc[i] = jnp.zeros((PORTS, FIL), f32)

    ready_sources(member * BLK, member * BLK)
    for copy in list_copies:
        copy.wait()
    twin_lists = remote(
        lists.at[pl.ds(0, MEMBERS)], lists.at[pl.ds(MEMBERS, MEMBERS)], t_send, t_recv, (twin, member)
    )
    twin_lists.start()
    pass_on(1)
    twin_lists.wait()
    li, lj, total = list_pairs(lists[...], member, core)
    table[0:LIST] = li
    table[LIST : 2 * LIST] = lj
    table[2 * LIST : 2 * LIST + 8] = jnp.broadcast_to(total, (8, 32))
    for step in (0, 2):
        unit_copies[step].wait_recv()
        ready_sources(mate_of(step) * BLK, mate_of(step) * BLK)
    pass_on(2)
    unit_copies[1].wait_recv()
    ready_sources(mate_of(1) * BLK, mate_of(1) * BLK)

    @pl.loop(0, BLK)
    def _(b):
        i = member * BLK + b
        for piece in tile_pieces(cols, i, blocks[i, 0:8, :], base, tile):
            piece()
        product = lax.dot_general(terms[i], tile[...], (((1,), (1,)), ((), ())), preferred_element_type=f32)
        acc[i] = fold(product, blocks[i, 3:6, :])

    from_core(0)
    ready_sources(SLAB + (1 - core) * BLK, SLAB)
    ready_partners(core * BLK, BLK)
    from_core(1)
    ready_partners(2 * BLK, 2 * BLK)
    pass_on(3)
    from_core(2)
    ready_partners(4 * BLK, 2 * BLK)
    ready_partners((6 + core) * BLK, BLK)
    from_core(3)
    ready_partners((7 - core) * BLK, BLK)
    for group_of in hops:
        for copy in group_of:
            copy.wait_send()
    for copy in unit_copies + list(core_copies.values()):
        copy.wait_send()


def fetch(*inputs):
    hbm = pl.BlockSpec(memory_space=pltpu.HBM)
    vm = pl.BlockSpec(memory_space=pltpu.VMEM)
    dma = pltpu.SemaphoreType.DMA
    return pl.pallas_call(
        fetch_kernel,
        out_shape=[
            jax.ShapeDtypeStruct((ALL, ROWS, FIL), f32),
            jax.ShapeDtypeStruct((ALL, 6 * PORTS, FIL), bf16),
            jax.ShapeDtypeStruct((SLAB + BLK, 4, FIL, 128), f32),
            jax.ShapeDtypeStruct((ALL + 1, PORTS, FIL), f32),
            jax.ShapeDtypeStruct((88, 32), jnp.int32),
        ],
        in_specs=[hbm] * 6,
        out_specs=[vm] * 5,
        scratch_shapes=[
            pltpu.VMEM((3, BLK * FIL), f32),
            pltpu.VMEM((3, BLK * FIL), f32),
            pltpu.VMEM((1, BLK * FIL), f32),
            pltpu.VMEM((PORTS, BLK * FIL), f32),
            pltpu.VMEM((BLK, MAXP), jnp.int32),
            pltpu.SMEM((BLK,), jnp.int32),
            dma((6,)),
            pltpu.VMEM((8, FIL), jnp.int32),
            pltpu.VMEM((FIL, FIL), bf16),
            dma, dma,
            dma((3,)), dma((3,)), dma((3,)), dma((3,)),
            dma((3, PARTS)), dma((3, PARTS)),
            dma((HOPS, PARTS)), dma((HOPS, PARTS)),
        ],
        compiler_params=pltpu.CompilerParams(
            collective_id=0, has_side_effects=True, vmem_limit_bytes=8 * 2**20
        ),
    )(*inputs)


def tiles_kernel(table, blocks, terms, cols, start, acc, even, odd, turns, sem):
    load = pltpu.make_async_copy(table, turns, sem)
    load.start()
    load.wait()
    n = turns[2 * LIST, 0]
    base = depth_base(lax.axis_index("wide"))

    def pair(k):
        row, col = k // 32, k & 31
        return turns[row, col], turns[LIST + row, col]

    def chunks(k, buf):
        i, j = pair(k)
        held = jnp.where(i < SLAB, i, SLAB + (i & (BLK - 1)))
        return tile_pieces(cols, held, blocks[jnp.minimum(j, ALL - 1), 0:8, :], base, buf)

    def step(k_next, buf_next, k, buf):
        work = chunks(k_next, buf_next)
        i_put, j_put = pair(k)
        i, j = jnp.minimum(i_put, ALL - 1), jnp.minimum(j_put, ALL - 1)
        behind = lax.dot_general(terms[i], buf[...], (((1,), (0,)), ((), ())), preferred_element_type=f32)
        for piece in work[:8]:
            piece()
        acc[j_put] += fold(behind, blocks[j, 3:6, :])
        ahead = lax.dot_general(terms[j], buf[...], (((1,), (1,)), ((), ())), preferred_element_type=f32)
        for piece in work[8:]:
            piece()
        acc[i_put] += fold(ahead, blocks[i, 3:6, :])

    for piece in chunks(0, even):
        piece()

    def steps(k, count):
        for q in range(count):
            now, later = (even, odd) if q % 2 == 0 else (odd, even)
            step(k + q + 1, later, k + q, now)

    half = UNROLL // 2

    @pl.loop(0, (n + half - 1) // UNROLL)
    def _(turn):
        steps(UNROLL * turn, UNROLL)

    left = n & (UNROLL - 1)

    @pl.when((left > 0) & (left <= half))
    def _():
        steps(n - left, half)


def tiles(table, blocks, terms, cols, acc):
    vm = pl.BlockSpec(memory_space=pltpu.VMEM)
    return pl.pallas_call(
        tiles_kernel,
        out_shape=jax.ShapeDtypeStruct((ALL + 1, PORTS, FIL), f32),
        in_specs=[vm] * 5,
        out_specs=vm,
        scratch_shapes=[
            pltpu.VMEM((FIL, FIL), bf16),
            pltpu.VMEM((FIL, FIL), bf16),
            pltpu.SMEM((88, 32), jnp.int32),
            pltpu.SemaphoreType.DMA,
        ],
        input_output_aliases={4: 0},
        compiler_params=pltpu.CompilerParams(vmem_limit_bytes=TILES_VMEM),
    )(table, blocks, terms, cols, acc)


def return_kernel(
    acc, out, x_buf, y_buf, z_buf, z_out, y_send, y_recv, z_send, z_recv, c_send, c_recv
):
    wide, member, core, twin, ahead, behind = place()
    mates = [lax.rem(member + step, MEMBERS) for step in range(1, MEMBERS)]
    first, last = wide < 2, wide >= lax.axis_size("wide") - 2
    barrier = pltpu.get_barrier_semaphore()
    for device in [(wide, mate) for mate in mates] + [(twin, member)]:
        pl.semaphore_signal(barrier, inc=1, device_id=device, device_id_type=MESH)

    @pl.when(~first)
    def _():
        pl.semaphore_signal(barrier, inc=1, device_id=(behind, member), device_id_type=MESH)

    pl.semaphore_wait(barrier, jnp.where(last, MEMBERS, MEMBERS + 1))
    half = BLK // PARTS
    core_copies = {}
    for hop in range(HOPS - 1, -1, -1):
        for part in range(PARTS):
            copy = remote(
                acc.at[pl.ds(SLAB + (2 * hop + 1 - core) * BLK + part * half, half)],
                x_buf.at[hop, pl.ds(part * half, half)],
                c_send.at[hop, part], c_recv.at[hop, part], (twin, member),
            )
            copy.start()
            core_copies[hop, part] = copy
    unit_copies = []
    for step, mate in enumerate(mates):
        copy = remote(
            acc.at[pl.ds(mate * BLK, BLK)], y_buf.at[step], y_send.at[step], y_recv.at[step], (wide, mate)
        )
        copy.start()
        unit_copies.append(copy)
    hops = {}
    for hop in range(HOPS - 1, -1, -1):
        for part in range(PARTS):
            cut = pl.ds(part * half, half)
            core_copies[hop, part].wait_recv()
            value = x_buf[hop, cut] + acc[pl.ds(SLAB + (2 * hop + core) * BLK + part * half, half)]
            if hop < HOPS - 1:
                @pl.when(~first)
                def _():
                    hops[hop + 1, part].wait_recv()

                value = value + jnp.where(first, 0.0, z_buf[hop, cut])
            if hop > 0:
                z_out[hop - 1, cut] = value
                copy = remote(
                    z_out.at[hop - 1, cut], z_buf.at[hop - 1, cut],
                    z_send.at[hop - 1, part], z_recv.at[hop - 1, part], (ahead, member),
                )
                hops[hop, part] = copy

                @pl.when(~last)
                def _():
                    copy.start()
            else:
                if part == 0:
                    for copy in unit_copies:
                        copy.wait_recv()
                value = value + acc[pl.ds(member * BLK + part * half, half)]
                for step in range(MEMBERS - 1):
                    value = value + y_buf[step, cut]
                for b in range(half):
                    at = (part * half + b) * FIL
                    out[:, at : at + FIL] = value[b]
    for copy in list(core_copies.values()) + unit_copies:
        copy.wait_send()

    @pl.when(~last)
    def _():
        for copy in hops.values():
            copy.wait_send()


def send_home(acc):
    vm = pl.BlockSpec(memory_space=pltpu.VMEM)
    dma = pltpu.SemaphoreType.DMA
    return pl.pallas_call(
        return_kernel,
        out_shape=jax.ShapeDtypeStruct((PORTS, BLK * FIL), f32),
        in_specs=[vm],
        out_specs=vm,
        scratch_shapes=[
            pltpu.VMEM((HOPS, BLK, PORTS, FIL), f32),
            pltpu.VMEM((MEMBERS - 1, BLK, PORTS, FIL), f32),
            pltpu.VMEM((HOPS - 1, BLK, PORTS, FIL), f32),
            pltpu.VMEM((HOPS - 1, BLK, PORTS, FIL), f32),
            dma((3,)), dma((3,)),
            dma((HOPS - 1, PARTS)), dma((HOPS - 1, PARTS)),
            dma((HOPS, PARTS)), dma((HOPS, PARTS)),
        ],
        compiler_params=pltpu.CompilerParams(
            collective_id=1, has_side_effects=True, vmem_limit_bytes=8 * 2**20
        ),
    )(acc)


def on_device(positions, directions, radius, currents, pair_target, pair_count):
    rad = radius.reshape(1, BLK * FIL)
    inputs = (positions, directions, rad, currents, pair_target, pair_count)
    inputs = [pltpu.with_memory_space_constraint(x, pltpu.HBM) for x in inputs]
    blocks, terms, cols, acc, table = fetch(*inputs)
    return send_home(tiles(table, blocks, terms, cols, acc))


def solution(mesh):
    return jax.shard_map(
        on_device,
        mesh=mesh,
        in_specs=(
            P(None, ("wide", "narrow")),
            P(None, ("wide", "narrow")),
            P(("wide", "narrow")),
            P(None, ("wide", "narrow")),
            P(("wide", "narrow"), None),
            P(("wide", "narrow")),
        ),
        out_specs=P(None, ("wide", "narrow")),
        check_vma=False,
    )
```
